32 devices in a mesh: seq: 8 (over y, x, core), fsdp: 4 (over z).
Axes of the slice: x: 2, y: 2, z: 4, core: 2. Of those that a mesh axis runs over, the one named last changes fastest.
Arguments:
- first_tier_source: bfloat16 [4, 8192, 768], P('fsdp', 'seq'), may hold values from -6 to 6
- token_articles: int32 [4, 8192], P('fsdp', 'seq'), may hold values from 0 to 3, as said below
- extra_spikes: float32 [4, 8192, 24], P('fsdp', 'seq'), may hold values from -0.7 to 0, as said below
- upstream_gradient: bfloat16 [4, 8192, 768], P('fsdp', 'seq'), may hold values from -6 to 6
- entering_projection: bfloat16 [2, 768, 3352], P(None, 'fsdp'), may hold values from -0.21875 to 0.21875
- exit_projection: bfloat16 [2, 1536, 768], P(None, 'fsdp'), may hold values from -0.15625 to 0.15625
- filter_kernels: bfloat16 [2, 4, 1792], P(None, None, 'fsdp'), may hold values from -3 to 3
- filter_shifts: bfloat16 [2, 1792], P(None, 'fsdp'), may hold values from -1.75 to 1.75
- stride_shifts: bfloat16 [2, 24], P(None, 'fsdp'), may hold values from -6.875 to -2.25
- log_shrink_rates: bfloat16 [2, 24], P(None, 'fsdp'), may hold values from -3 to 2.765625
- bypass_coefficient: bfloat16 [2, 24], P(None, 'fsdp'), may hold values from 0.5 to 1.5
- entry_scaling_gains: bfloat16 [2, 768], P(None, 'fsdp'), may hold values from 0.5 to 1.5
- gated_scaling_gains: bfloat16 [2, 1536], P(None, 'fsdp'), may hold values from 0.5 to 1.5
Outputs:
- outputs: bfloat16 [4, 8192, 768], P('fsdp', 'seq')
- input_grad: float32 [4, 8192, 768], P('fsdp', 'seq')
- grad_in_weight: float32 [2, 768, 3352], P(None, 'fsdp')
- grad_out_weight: float32 [2, 1536, 768], P(None, 'fsdp')
- grad_conv_weight: float32 [2, 4, 1792], P(None, None, 'fsdp')
- grad_conv_bias: float32 [2, 1792], P(None, 'fsdp')
- grad_step_bias: float32 [2, 24], P(None, 'fsdp')
- grad_decay_log: float32 [2, 24], P(None, 'fsdp')
- grad_skip_gain: float32 [2, 24], P(None, 'fsdp')
- grad_norm_gain: float32 [2, 768], P(None, 'fsdp')
- grad_gate_gain: float32 [2, 1536], P(None, 'fsdp')
The draws below stay inside these ranges and needn't reach their ends.
Inputs may be any that keep to these rules, and one draw needn't show every extreme that they name: `token_articles`: document numbers never fall along a sequence. In one sequence, drawn from the seed, one document begins on the first device of seq and ends on the last; in every other sequence documents begin exactly at the first tokens of the two middle devices of seq. `extra_spikes`: zero except at a few positions of each sequence, where every head gets its own negative value.
All inputs are finite; a program needn't handle non-finite values.
Results may differ from the reference program's by a relative error of at most 0.02.
Values may be sent and summed in bfloat16 or wider, within the bound.
No kernel may reach another device: no remote copies, remote signals or barrier semaphores. Data moves between devices by JAX's collectives and lax.ppermute only.
A program may use at most 384 MiB of HBM per device.

```python
import jax
import jax.numpy as jnp
from jax import lax

D = 768
H = 24
P_SIZE = 64
N = 128
K = 4
CH = 256
LAYERS = 2
TOK_DEV = 1024
E = 1536
CV = 1792
PROJ = 3352
TOKEN_SPAN = 8192
SERIES_COUNT = 4
N_SEQ = 8


def draw_token_articles(key, part):
    key = jax.random.fold_in(key, 11)
    key_first, key_second, key_third, key_pick, key_tail = jax.random.split(key, 5)
    first_cut = jax.random.randint(key_first, (SERIES_COUNT, 1), 1, TOK_DEV)
    second_cut = TOKEN_SPAN - jax.random.randint(key_second, (SERIES_COUNT, 1), 1, TOK_DEV)
    third_cut = second_cut + jax.random.randint(key_third, (SERIES_COUNT, 1), 0, TOKEN_SPAN - second_cut)
    middle_first = jnp.full((SERIES_COUNT, 1), (N_SEQ // 2 - 1) * TOK_DEV, jnp.int32)
    middle_second = jnp.full((SERIES_COUNT, 1), N_SEQ // 2 * TOK_DEV, jnp.int32)
    tail_cut = TOKEN_SPAN - jax.random.randint(key_tail, (SERIES_COUNT, 1), 1, TOK_DEV)
    spanning = jax.random.randint(key_pick, (), 0, SERIES_COUNT)
    is_span = jnp.arange(SERIES_COUNT)[:, None] == spanning
    cut_one = jnp.where(is_span, first_cut, middle_first)
    cut_two = jnp.where(is_span, second_cut, middle_second)
    cut_three = jnp.where(is_span, third_cut, tail_cut)
    position = jnp.arange(TOKEN_SPAN)[None, :]
    return (position >= cut_one).astype(jnp.int32) + (position >= cut_two).astype(jnp.int32) + (position >= cut_three).astype(jnp.int32)


def draw_extra_spikes(key, part):
    key = jax.random.fold_in(key, 23)
    seed_location, key_size = jax.random.split(key)
    spike_chance = 3.0
    chosen_entry = jax.random.uniform(seed_location, (SERIES_COUNT, TOKEN_SPAN, 1)) < spike_chance / TOKEN_SPAN
    sizes_drawn = jax.random.uniform(key_size, (SERIES_COUNT, TOKEN_SPAN, H), jnp.float32, -0.7, -0.22)
    return jnp.where(chosen_entry, sizes_drawn, 0.0).astype(jnp.float32)


def shard_levels(own_key, dims, pieces, low, largest):
    level = 1.0
    for axis_at, shards_of in pieces:
        steps = jax.random.uniform(jax.random.fold_in(jax.random.fold_in(own_key, 6), axis_at), (shards_of,), jnp.float32, low / len(pieces), largest / len(pieces))
        level = level * jnp.repeat(jnp.exp(steps), dims[axis_at] // shards_of).reshape((-1,) + (1,) * (len(dims) - 1 - axis_at))
    return level


def scatter_about(own_key, extent, scale, bound, cuts=(), held_as=jnp.bfloat16):
    values = jax.random.normal(own_key, extent, jnp.float32) * scale
    if len(cuts) > 0:
        values = shard_levels(own_key, extent, cuts, -0.22, 0.18) * values
    return jnp.clip(values, min=-bound, max=bound).astype(held_as)


def setup_inputs(seed: int = 0) -> dict:
    streams_of = jax.random.split(jax.random.key(seed), 14)
    return {
        "first_tier_source": scatter_about(streams_of[0], (SERIES_COUNT, TOKEN_SPAN, D), 1.0, 6.0, ((0, 4), (1, 8))),
        "token_articles": draw_token_articles(jax.random.fold_in(streams_of[13], 71), 0),
        "extra_spikes": draw_extra_spikes(jax.random.fold_in(streams_of[13], 71), 0),
        "upstream_gradient": scatter_about(streams_of[3], (SERIES_COUNT, TOKEN_SPAN, D), 1.0, 6.0, ((0, 4), (1, 8))),
        "entering_projection": scatter_about(streams_of[4], (LAYERS, D, PROJ), D ** -0.5, 0.21875, ((1, 4),)),
        "exit_projection": scatter_about(streams_of[5], (LAYERS, E, D), E ** -0.5, 0.15625, ((1, 4),)),
        "filter_kernels": scatter_about(streams_of[6], (LAYERS, K, CV), K ** -0.5, 3.0, ((2, 4),)),
        "filter_shifts": scatter_about(streams_of[7], (LAYERS, CV), 0.3, 1.75, ((1, 4),)),
        "stride_shifts": jnp.clip(-6.875 + 4.625 * jax.random.uniform(streams_of[8], (LAYERS, H), jnp.float32) ** shard_levels(streams_of[8], (LAYERS, H), ((1, 4),), -0.2, 0.2), -6.875, -2.25).astype(jnp.bfloat16),
        "log_shrink_rates": jnp.clip(-3.0 + 5.765625 * jax.random.uniform(streams_of[9], (LAYERS, H), jnp.float32) ** shard_levels(streams_of[9], (LAYERS, H), ((1, 4),), -0.2, 0.2), -3.0, 2.765625).astype(jnp.bfloat16),
        "bypass_coefficient": jnp.clip(0.5 + 1.0 * jax.random.uniform(streams_of[10], (LAYERS, H), jnp.float32) ** shard_levels(streams_of[10], (LAYERS, H), ((1, 4),), -0.2, 0.2), 0.5, 1.5).astype(jnp.bfloat16),
        "entry_scaling_gains": jnp.clip(1.0 + 0.1 * jax.random.normal(streams_of[11], (LAYERS, D), jnp.float32), 0.5, 1.5).astype(jnp.bfloat16),
        "gated_scaling_gains": jnp.clip(1.0 + 0.1 * jax.random.normal(streams_of[12], (LAYERS, E), jnp.float32), 0.5, 1.5).astype(jnp.bfloat16),
    }


@jax.custom_vjp
def low(v):
    return lax.optimization_barrier(v.astype(jnp.bfloat16)).astype(jnp.float32)

@jax.custom_vjp
def low_back(v):
    return v

def low_keep(v):
    return (low(v), None)

def low_pass(kept, grad):
    return (grad,)

def back_keep(v):
    return (v, None)

def back_low(kept, grad):
    return (low(grad),)
low.defvjp(low_keep, low_pass)
low_back.defvjp(back_keep, back_low)
eps = 1e-05
highest = lax.Precision.HIGHEST

def product(left, right):
    return jnp.dot(left, right, precision=highest, preferred_element_type=jnp.float32)

def norm_input(running_activation, gain_vec):
    return running_activation * lax.rsqrt(lax.optimization_barrier(jnp.mean(running_activation * running_activation, axis=-1, keepdims=True)) + eps) * gain_vec

def gated_norm(mixed_out, gate_proj, gain_vec):
    gated = mixed_out * jax.nn.silu(gate_proj)
    return gated * lax.rsqrt(lax.optimization_barrier(jnp.mean(gated * gated, axis=-1, keepdims=True)) + eps) * gain_vec

def conv_mix(extended, article_widened, filter_kernel_entry, filter_shift_term):
    taps_count = filter_kernel_entry.shape[0]
    row_count = extended.shape[0] - taps_count + 1
    own_doc = article_widened[taps_count - 1:]
    mix_total = filter_shift_term
    for offset in range(taps_count):
        same_doc = (article_widened[offset:offset + row_count] == own_doc).astype(jnp.float32)[:, None]
        mix_total = mix_total + filter_kernel_entry[offset] * extended[offset:offset + row_count] * same_doc
    return mix_total

def build_sources(filter_source, edge_series, unscaled_stride, filter_kernel_entry, filter_shift_term, stride_shift, shrink_multiplier, article_widened, spike_log_rate):
    extended = jnp.concatenate([edge_series, filter_source])
    activated = jax.nn.silu(conv_mix(extended, article_widened, filter_kernel_entry, filter_shift_term))
    channel_group_source = activated[:, :E].reshape(activated.shape[0], H, P_SIZE)
    arriving_memory = activated[:, E:E + N]
    leaving_memory = activated[:, E + N:]
    stride_magnitude = jax.nn.softplus(unscaled_stride + stride_shift)
    shrink_log_rate = spike_log_rate - stride_magnitude * jnp.exp(shrink_multiplier)
    return (channel_group_source, arriving_memory, leaving_memory, stride_magnitude, shrink_log_rate)

def group_math(prior_state, seg_prior, channel_group_source, arriving_memory, leaving_memory, stride_magnitude, shrink_log_rate, article_number):
    length = article_number.shape[0]
    cum_log = jnp.cumsum(shrink_log_rate, axis=0)
    order_mask = jnp.arange(length)[:, None] >= jnp.arange(length)[None, :]
    kept_mask = (order_mask & (article_number[:, None] == article_number[None, :]))[:, :, None]
    gap_log = jnp.where(kept_mask, cum_log[:, None, :] - cum_log[None, :, :], 0.0)
    decay_mat = jnp.where(kept_mask, jnp.exp(gap_log), 0.0)
    scores = jnp.dot(leaving_memory, arriving_memory.T, precision=highest, preferred_element_type=jnp.float32)
    mixing = decay_mat * scores[:, :, None] * stride_magnitude[None, :, :]
    result = jnp.einsum('ijh,jhp->ihp', mixing, channel_group_source, precision=highest)
    start_gain = (article_number == seg_prior).astype(jnp.float32)[:, None] * jnp.exp(cum_log)
    result = result + start_gain[:, :, None] * jnp.einsum('in,hpn->ihp', leaving_memory, prior_state, precision=highest)
    tail_gain = (article_number == article_number[-1]).astype(jnp.float32)[:, None] * jnp.exp(cum_log[-1][None, :] - cum_log) * stride_magnitude
    carried = jnp.exp(cum_log[-1]) * (article_number[-1] == seg_prior).astype(jnp.float32)
    new_state = carried[:, None, None] * prior_state + jnp.einsum('jh,jhp,jn->hpn', tail_gain, channel_group_source, arriving_memory, precision=highest)
    return (new_state, result)

def local_scan(channel_group_source, arriving_memory, leaving_memory, stride_magnitude, shrink_log_rate, article_number, seg_before):
    block_count = channel_group_source.shape[0] // CH

    def to_blocks(array_in):
        return array_in.reshape((block_count, CH) + array_in.shape[1:])
    prior_ids = jnp.concatenate([jnp.reshape(seg_before, (1,)).astype(jnp.int32), article_number[:-1].astype(jnp.int32)])
    starts = to_blocks(prior_ids)[:, 0]

    def one_block(prior_state, partition_parts):
        return group_math(prior_state, *partition_parts)
    zero_state = jnp.zeros((channel_group_source.shape[1], channel_group_source.shape[2], arriving_memory.shape[1]), jnp.float32)
    final_state, block_out = lax.scan(jax.checkpoint(one_block), zero_state, (starts, to_blocks(channel_group_source), to_blocks(arriving_memory), to_blocks(leaving_memory), to_blocks(stride_magnitude), to_blocks(shrink_log_rate), to_blocks(article_number)))
    return (final_state, block_out.reshape(channel_group_source.shape))

def mamba_tier(running_activation, article_number, spike_log_rate, model_tensors):
    in_mat, out_mat, filter_kernel_entry, filter_shift_term, stride_shift, shrink_multiplier, skip_vec, gain_in, gain_out = model_tensors
    normed = low(norm_input(running_activation, gain_in))
    projected = low_back(product(normed, in_mat))
    gate_proj = projected[:, :E]
    filter_source = projected[:, E:E + CV]
    unscaled_stride = projected[:, E + CV:]
    edge_series = jnp.zeros((K - 1, CV), jnp.float32)
    article_widened = jnp.concatenate([jnp.full((K - 1,), -1, jnp.int32), article_number.astype(jnp.int32)])
    channel_group_source, arriving_memory, leaving_memory, stride_magnitude, shrink_log_rate = build_sources(filter_source, edge_series, unscaled_stride, filter_kernel_entry, filter_shift_term, stride_shift, shrink_multiplier, article_widened, spike_log_rate)
    final_state, local_out = local_scan(channel_group_source, arriving_memory, leaving_memory, stride_magnitude, shrink_log_rate, article_number, jnp.int32(-1))
    mixed_out = local_out + skip_vec[:, None] * channel_group_source
    out_normed = low(gated_norm(mixed_out.reshape(mixed_out.shape[0], E), gate_proj, gain_out))
    return running_activation + low_back(product(out_normed, out_mat))

def reference(first_tier_source, token_articles, extra_spikes, upstream_gradient, entering_projection, exit_projection, filter_kernels, filter_shifts, stride_shifts, log_shrink_rates, bypass_coefficient, entry_scaling_gains, gated_scaling_gains):
    model_tensors = tuple((array_in.astype(jnp.float32) for array_in in (entering_projection, exit_projection, filter_kernels, filter_shifts, stride_shifts, log_shrink_rates, bypass_coefficient, entry_scaling_gains, gated_scaling_gains)))

    def forward(complete_source, trainable_tensors):

        def lone_series(partition_parts):
            running_activation, article_number, spike_log_rate = partition_parts
            for tier_number in range(LAYERS):
                running_activation = mamba_tier(running_activation, article_number, spike_log_rate, tuple((partition_owner[tier_number] for partition_owner in trainable_tensors)))
            return running_activation
        return lax.map(lone_series, (complete_source, token_articles, extra_spikes.astype(jnp.float32)))
    result, pullback = jax.vjp(forward, first_tier_source.astype(jnp.float32), model_tensors)
    grad_x, grads = pullback(upstream_gradient.astype(jnp.float32))
    return (result.astype(jnp.bfloat16), grad_x, grads[0], grads[1], grads[2], grads[3], grads[4], grads[5], grads[6], grads[7], grads[8])
```

```python
import jax
import jax.numpy as jnp
import numpy as np
from jax import lax
from jax.experimental import pallas as pl
from jax.experimental.pallas import tpu as pltpu
from jax.sharding import PartitionSpec as P

D = 768
H = 24
P_SIZE = 64
N = 128
K = 4
E = 1536
CV = 1792
CX = CV + 128
Q = 128
TT = 256
SUB = TT // Q
W = 256
HP = 32
PAIRS = H // 2
eps = 1e-05
LOG2E = 1.4426950408889634
BIG = -1e30
CUT = 30000.0
f32 = jnp.float32
bf16 = jnp.bfloat16
highest = lax.Precision.HIGHEST
VMEM_LIMIT = 56 * 1024 * 1024


def nn(a, b):
    return lax.dot_general(a, b, (((1,), (0,)), ((), ())), preferred_element_type=f32)


def nt(a, b):
    return lax.dot_general(a, b, (((1,), (1,)), ((), ())), preferred_element_type=f32)


def tn(a, b):
    return lax.dot_general(a, b, (((0,), (0,)), ((), ())), preferred_element_type=f32)


def nn_exact(a, b):
    return lax.dot_general(
        a, b, (((1,), (0,)), ((), ())), precision=highest, preferred_element_type=f32
    )


def halves(v):
    hi = v.astype(bf16)
    lo = (v - hi.astype(f32)).astype(bf16)
    return jnp.concatenate([hi, lo], axis=1)


def sigmoid(v):
    return 0.5 + 0.5 * jnp.tanh(0.5 * v)


def softplus(v):
    return jnp.maximum(v, 0.0) + jnp.log1p(jnp.exp(-jnp.abs(v)))


def iota2(shape, dim):
    return lax.broadcasted_iota(jnp.int32, shape, dim)


def lane_halves():
    lane = iota2((1, 2 * P_SIZE), 1)
    left = (lane < P_SIZE).astype(f32).astype(bf16)
    right = (lane >= P_SIZE).astype(f32).astype(bf16)
    return left, right


def full(shape):
    return pl.BlockSpec(shape, lambda i: (0,) * len(shape))


def rows(width, size=TT):
    return pl.BlockSpec((size, width), lambda i: (i, 0))


def cols(height):
    return pl.BlockSpec((height, TT), lambda i: (0, i))


def params():
    return pltpu.CompilerParams(vmem_limit_bytes=VMEM_LIMIT, dimension_semantics=("arbitrary",))


def shape(dims, dtype):
    return jax.ShapeDtypeStruct(dims, dtype)


def project_kernel(x_ref, gain_ref, w_ref, normed_ref, xc_ref, dtr_ref):
    x = x_ref[...].astype(f32)
    scale = lax.rsqrt(jnp.mean(x * x, axis=-1, keepdims=True) + eps)
    normed = (x * scale * gain_ref[...]).astype(bf16)
    normed_ref[...] = normed
    xc_ref[...] = nn(normed, w_ref[:, :CV]).astype(bf16)
    dtr_ref[...] = nn(normed, w_ref[:, CV:])


def project(x, gain, w):
    t = x.shape[0]
    return pl.pallas_call(
        project_kernel,
        grid=(t // TT,),
        in_specs=[rows(D), full((1, D)), full((D, CX))],
        out_specs=[rows(D), rows(CV), rows(128)],
        out_shape=[shape((t, D), bf16), shape((t, CV), bf16), shape((t, 128), f32)],
        compiler_params=params(),
        name="project",
    )(x, gain, w)


def gate_kernel(normed_ref, w_ref, z_ref):
    z_ref[...] = nn(normed_ref[...], w_ref[...]).astype(bf16)


def project_gate(normed, w):
    t = normed.shape[0]
    return pl.pallas_call(
        gate_kernel,
        grid=(t // TT,),
        in_specs=[rows(D), full((D, E))],
        out_specs=rows(E),
        out_shape=shape((t, E), bf16),
        compiler_params=params(),
        name="project_gate",
    )(normed, w)


def prepare_kernel(
    xc_ref, edge_ref, cw_ref, dtr_ref, spike_ref, tok_ref, pv_ref, e2_ref,
    pre_ref, x_ref, bc_ref, dt_ref, cum_ref, cumt_ref, dtt_ref, packed_ref,
    ext, state_ref, carry_ref,
):
    step = pl.program_id(0)

    @pl.when(step == 0)
    def _():
        ext[0:8, :] = edge_ref[...]
        state_ref[...] = jnp.zeros_like(state_ref)
        carry_ref[...] = jnp.zeros_like(carry_ref)

    @pl.when(step > 0)
    def _():
        ext[0:8, :] = ext[TT : TT + 8, :]

    ext[8 : TT + 8, :] = xc_ref[...].astype(f32)
    masks = [tok_ref[:, k : k + 1] for k in range(K - 1)]
    for b in range(CV // 128):
        at = slice(b * 128, (b + 1) * 128)
        total = cw_ref[K : K + 1, at] + cw_ref[K - 1 : K, at] * ext[8 : TT + 8, at]
        for k in range(K - 1):
            total = total + cw_ref[k : k + 1, at] * (ext[5 + k : 5 + k + TT, at] * masks[k])
        pre_ref[:, at] = total.astype(bf16)
        act = (total * sigmoid(total)).astype(bf16)
        if b < E // 128:
            x_ref[:, at] = act
        else:
            bc_ref[:, (b - E // 128) * 128 : (b - E // 128 + 1) * 128] = act

    dt = softplus(dtr_ref[...] + pv_ref[0:1, :])
    log_decay = (spike_ref[...] - dt * pv_ref[1:2, :]) * LOG2E
    dt_ref[...] = dt
    dtt_ref[...] = jnp.transpose(dt)[:HP, :]
    lower = (iota2((Q, Q), 0) >= iota2((Q, Q), 1)).astype(f32)
    for s in range(SUB):
        r = slice(s * Q, (s + 1) * Q)
        cum = nn_exact(lower, log_decay[r])
        cum_ref[r, :] = cum
        cumt_ref[:, r] = jnp.transpose(cum)[:HP, :]
        last = cum[Q - 1 : Q, :]
        tail = jnp.exp2(last - cum) * tok_ref[r, 7:8] * dt[r]
        kept = tok_ref[s * Q + Q - 1 : s * Q + Q, 6:7]
        carried = jnp.exp2(last) * kept
        carry_ref[...] = carry_ref[...] + (last + (kept - 1.0) * CUT)
        wide = jnp.concatenate([tail, jnp.broadcast_to(carried, (16, 128))], axis=0)
        wide = halves(wide)
        b_in = bc_ref[r, :N]
        for b in range(E // W):
            at = slice(b * W, (b + 1) * W)
            grown = nn(wide, e2_ref[:, at])
            weighted = (x_ref[r, at].astype(f32) * grown[:Q]).astype(bf16)
            state_ref[:, at] = state_ref[:, at] * grown[Q : Q + 1] + tn(b_in, weighted)

    @pl.when(step == pl.num_programs(0) - 1)
    def _():
        packed_ref[:N, :] = state_ref[...].astype(bf16)
        packed_ref[N:, :] = jnp.zeros((16, E), bf16)
        rest = jnp.concatenate([carry_ref[...], carry_ref[...]], axis=0)
        for k in range(3):
            part = rest.astype(bf16)
            packed_ref[N:, k * 128 : (k + 1) * 128] = part
            rest = rest - part.astype(f32)


def prepare(xc, edge, cw, dtr, spike, tok, pv, e2):
    t = xc.shape[0]
    return pl.pallas_call(
        prepare_kernel,
        grid=(t // TT,),
        in_specs=[
            rows(CV), full((8, CV)), full((8, CV)), rows(128), rows(128), rows(128),
            full((8, 128)), full((256, E)),
        ],
        out_specs=[
            rows(CV), rows(E), rows(2 * N), rows(128), rows(128), cols(HP), cols(HP),
            full((N + 16, E)),
        ],
        out_shape=[
            shape((t, CV), bf16),
            shape((t, E), bf16),
            shape((t, 2 * N), bf16),
            shape((t, 128), f32),
            shape((t, 128), f32),
            shape((HP, t), f32),
            shape((HP, t), f32),
            shape((N + 16, E), bf16),
        ],
        scratch_shapes=[
            pltpu.VMEM((TT + 8, CV), f32),
            pltpu.VMEM((N, E), f32),
            pltpu.VMEM((8, 128), f32),
        ],
        compiler_params=params(),
        name="prepare",
    )(xc, edge, cw, dtr, spike, tok, pv, e2)


def within_kernel(x_ref, bc_ref, cum_ref, cumt_ref, dtt_ref, tok_ref, doct_ref, y_ref):
    left, right = lane_halves()
    order = iota2((Q, Q), 0) >= iota2((Q, Q), 1)
    for s in range(SUB):
        r = slice(s * Q, (s + 1) * Q)
        same = tok_ref[r, 8:9] == doct_ref[0:1, r]
        bias = jnp.where(order & same, 0.0, BIG)
        scores = nt(bc_ref[r, N:], bc_ref[r, :N])
        cum = cum_ref[r, :]
        for p in range(PAIRS):
            at = slice(p * 128, (p + 1) * 128)
            xp = x_ref[r, at]
            mixes = []
            for h in (2 * p, 2 * p + 1):
                gap = (cum[:, h : h + 1] - cumt_ref[h : h + 1, r]) + bias
                mixes.append((jnp.exp2(gap) * (scores * dtt_ref[h : h + 1, r])).astype(bf16))
            both = jnp.concatenate([xp * left, xp * right], axis=0)
            y_ref[r, at] = nn(jnp.concatenate(mixes, axis=1), both).astype(bf16)


def within(x, bc, cum, cumt, dtt, tok, doct):
    t = x.shape[0]
    return pl.pallas_call(
        within_kernel,
        grid=(t // TT,),
        in_specs=[rows(E), rows(2 * N), rows(128), cols(HP), cols(HP), rows(128), cols(8)],
        out_specs=rows(E),
        out_shape=shape((t, E), bf16),
        compiler_params=params(),
        name="within",
    )(x, bc, cum, cumt, dtt, tok, doct)


def across_kernel(
    yi_ref, x_ref, bc_ref, dt_ref, cum_ref, tok_ref, z_ref, first_ref, skip_ref, gain_ref,
    w_ref, res_ref, e2_ref,
    y_ref, low_ref, new_ref, prior_ref,
    state, gated,
):
    step = pl.program_id(0)

    @pl.when(step == 0)
    def _():
        state[...] = first_ref[...]

    for s in range(SUB):
        r = slice(s * Q, (s + 1) * Q)
        cum = cum_ref[r, :]
        last = cum[Q - 1 : Q, :]
        tail = jnp.exp2(last - cum) * tok_ref[r, 7:8] * dt_ref[r, :]
        head = jnp.exp2(cum) * tok_ref[r, 6:7]
        carried = head[Q - 1 : Q, :]
        wide = halves(
            jnp.concatenate([tail, head, jnp.broadcast_to(carried, (16, 128))], axis=0)
        )
        b_in = bc_ref[r, :N]
        c_out = bc_ref[r, N:]
        square = jnp.zeros((Q, W), f32)
        for b in range(E // W):
            at = slice(b * W, (b + 1) * W)
            grown = nn(wide, e2_ref[:, at])
            xs = x_ref[r, at].astype(f32)
            held = state[:, at]
            prior_ref[s, :, at] = held.astype(bf16)
            y = (
                yi_ref[r, at].astype(f32)
                + nn(c_out, held.astype(bf16)) * grown[Q : 2 * Q]
                + skip_ref[0:1, at] * xs
            )
            y_ref[r, at] = y.astype(bf16)
            z = z_ref[r, at].astype(f32)
            made = y * (z * sigmoid(z))
            gated[r, at] = made
            square = square + made * made
            weighted = (xs * grown[:Q]).astype(bf16)
            state[:, at] = held * grown[2 * Q : 2 * Q + 1] + tn(b_in, weighted)
        scale = lax.rsqrt(jnp.sum(square, axis=-1, keepdims=True) * (1.0 / E) + eps)
        for b in range(E // W):
            at = slice(b * W, (b + 1) * W)
            low_ref[r, at] = (gated[r, at] * scale * gain_ref[0:1, at]).astype(bf16)
    new = res_ref[...].astype(f32) + nn(low_ref[...], w_ref[...])
    new_ref[...] = new.astype(new_ref.dtype)


def across(yi, x, bc, dt, cum, tok, z, first, skip, gain, w, res, e2, out_type):
    t = x.shape[0]
    return pl.pallas_call(
        across_kernel,
        grid=(t // TT,),
        in_specs=[
            rows(E), rows(E), rows(2 * N), rows(128), rows(128), rows(128), rows(E),
            full((N, E)), full((1, E)), full((1, E)), full((E, D)), rows(D), full((256, E)),
        ],
        out_specs=[rows(E), rows(E), rows(D), pl.BlockSpec((SUB, N, E), lambda i: (i, 0, 0))],
        out_shape=[
            shape((t, E), bf16),
            shape((t, E), bf16),
            shape((t, D), out_type),
            shape((t // Q, N, E), bf16),
        ],
        scratch_shapes=[pltpu.VMEM((N, E), f32), pltpu.VMEM((TT, E), f32)],
        compiler_params=params(),
        name="across",
    )(yi, x, bc, dt, cum, tok, z, first, skip, gain, w, res, e2)


def open_back_kernel(
    g_ref, w_ref, y_ref, z_ref, x_ref, bc_ref, cum_ref, tok_ref, gain_ref, e2_ref,
    dy_ref, dz_ref, gb_ref, acc_ref, low_ref,
    held, state_ref,
):
    step = pl.program_id(0)

    @pl.when(step == 0)
    def _():
        acc_ref[...] = jnp.zeros_like(acc_ref)
        state_ref[...] = jnp.zeros_like(state_ref)

    gb = g_ref[...].astype(bf16)
    gb_ref[...] = gb
    held[...] = nt(gb, w_ref[...])
    for s in reversed(range(SUB)):
        r = slice(s * Q, (s + 1) * Q)
        square = jnp.zeros((Q, W), f32)
        cross = jnp.zeros((Q, W), f32)
        for b in range(E // W):
            at = slice(b * W, (b + 1) * W)
            z = z_ref[r, at].astype(f32)
            gated = y_ref[r, at].astype(f32) * (z * sigmoid(z))
            square = square + gated * gated
            cross = cross + gated * (held[r, at] * gain_ref[0:1, at])
        scale = lax.rsqrt(jnp.sum(square, axis=-1, keepdims=True) * (1.0 / E) + eps)
        pull = (scale * scale * scale) * (jnp.sum(cross, axis=-1, keepdims=True) * (1.0 / E))
        cum = cum_ref[r, :]
        head = jnp.exp2(cum) * tok_ref[r, 6:7]
        wide = halves(
            jnp.concatenate([head, jnp.broadcast_to(head[Q - 1 : Q, :], (16, 128))], axis=0)
        )
        c_out = bc_ref[r, N:]
        for b in range(E // W):
            at = slice(b * W, (b + 1) * W)
            z = z_ref[r, at].astype(f32)
            gate = sigmoid(z)
            y = y_ref[r, at].astype(f32)
            gated = y * (z * gate)
            dn = held[r, at]
            acc_ref[0:1, at] += jnp.sum(dn * (gated * scale), axis=0, keepdims=True)
            dgated = scale * (dn * gain_ref[0:1, at]) - gated * pull
            dy = dgated * (z * gate)
            dz_ref[r, at] = (dgated * y * (gate * (1.0 + z * (1.0 - gate)))).astype(bf16)
            acc_ref[1:2, at] += jnp.sum(dy * x_ref[r, at].astype(f32), axis=0, keepdims=True)
            dy_ref[r, at] = dy.astype(bf16)
            grown = nn(wide, e2_ref[:, at])
            state_ref[:, at] = state_ref[:, at] * grown[Q : Q + 1] + tn(
                c_out, (dy * grown[:Q]).astype(bf16)
            )

    @pl.when(step == pl.num_programs(0) - 1)
    def _():
        low_ref[...] = state_ref[...].astype(bf16)


def open_back(g, w, y, z, x, bc, cum, tok, gain, e2):
    t = x.shape[0]
    n = t // TT

    def turned(width):
        return pl.BlockSpec((TT, width), lambda i: (n - 1 - i, 0))

    return pl.pallas_call(
        open_back_kernel,
        grid=(n,),
        in_specs=[
            turned(D), full((E, D)), turned(E), turned(E), turned(E), turned(2 * N),
            turned(128), turned(128), full((1, E)), full((256, E)),
        ],
        out_specs=[turned(E), turned(E), turned(D), full((8, E)), full((N, E))],
        out_shape=[
            shape((t, E), bf16),
            shape((t, E), bf16),
            shape((t, D), bf16),
            shape((8, E), f32),
            shape((N, E), bf16),
        ],
        scratch_shapes=[pltpu.VMEM((TT, E), f32), pltpu.VMEM((N, E), f32)],
        compiler_params=params(),
        name="open_back",
    )(g, w, y, z, x, bc, cum, tok, gain, e2)


def within_back_kernel(
    x_ref, dy_ref, bc_ref, dt_ref, cum_ref, cumt_ref, tok_ref, doct_ref, hot_ref, sel_ref,
    dxdt_ref, dbc_ref, cross_ref,
):
    left, right = lane_halves()
    order = iota2((Q, Q), 1) >= iota2((Q, Q), 0)
    suffix = order.astype(f32)
    for s in range(SUB):
        r = slice(s * Q, (s + 1) * Q)
        same = tok_ref[r, 8:9] == doct_ref[0:1, r]
        bias = jnp.where(order & same, 0.0, BIG)
        b_in = bc_ref[r, :N]
        c_out = bc_ref[r, N:]
        scores = nt(b_in, c_out)
        cum = cum_ref[r, :]
        dt = dt_ref[r, :]
        grad_scores = jnp.zeros((Q, Q), f32)
        by_source = jnp.zeros((Q, 128), f32)
        by_target = jnp.zeros((HP, Q), f32)
        for p in range(PAIRS):
            at = slice(p * 128, (p + 1) * 128)
            xp = x_ref[r, at]
            dyp = dy_ref[r, at]
            dmix = nt(jnp.concatenate([xp * left, xp * right], axis=0), dyp)
            mixes = []
            flows = []
            for i in range(2):
                h = 2 * p + i
                decay = jnp.exp2((cumt_ref[h : h + 1, r] - cum[:, h : h + 1]) + bias)
                mixes.append((decay * scores).astype(bf16))
                part = dmix[i * Q : (i + 1) * Q] * (decay * dt[:, h : h + 1])
                grad_scores = grad_scores + part
                flows.append((part * scores).astype(bf16))
            both = jnp.concatenate([dyp * left, dyp * right], axis=0)
            dxdt_ref[r, at] = nn(jnp.concatenate(mixes, axis=1), both).astype(bf16)
            by_source = by_source + nn(jnp.concatenate(flows, axis=1), hot_ref[p])
            by_target = by_target + nn(sel_ref[p], jnp.concatenate(flows, axis=0))
        low = grad_scores.astype(bf16)
        dbc_ref[r, :N] = nn(low, c_out)
        dbc_ref[r, N:] = tn(low, b_in)
        target = jnp.transpose(
            jnp.concatenate([by_target, jnp.zeros((128 - HP, Q), f32)], axis=0)
        )
        cross_ref[r, :] = nn_exact(suffix, target - by_source)


def within_back(x, dy, bc, dt, cum, cumt, tok, doct, hot, sel):
    t = x.shape[0]
    return pl.pallas_call(
        within_back_kernel,
        grid=(t // TT,),
        in_specs=[
            rows(E), rows(E), rows(2 * N), rows(128), rows(128), cols(HP), rows(128), cols(8),
            full(hot.shape), full(sel.shape),
        ],
        out_specs=[rows(E), rows(2 * N), rows(128)],
        out_shape=[shape((t, E), bf16), shape((t, 2 * N), f32), shape((t, 128), f32)],
        compiler_params=params(),
        name="within_back",
    )(x, dy, bc, dt, cum, cumt, tok, doct, hot, sel)


def across_back_kernel(
    x_ref, pre_ref, xc_ref, halo_ref, edge_ref, bc_ref, dy_ref, dxdt_ref, dbc_ref, cross_ref,
    dt_ref, cum_ref, dtr_ref, tok_ref, prior_ref, last_ref, skip_ref, cw_ref, pv_ref, e2_ref,
    et_ref,
    dxc_ref, cacc_ref, hacc_ref, first_ref,
    state, dp, ext,
):
    step = pl.program_id(0)
    count = pl.num_programs(0)

    @pl.when(step == 0)
    def _():
        state[...] = last_ref[...]
        cacc_ref[...] = jnp.zeros_like(cacc_ref)
        hacc_ref[...] = jnp.zeros_like(hacc_ref)
        dp[TT : TT + 8, :] = jnp.zeros((8, CV), f32)

    @pl.when(step > 0)
    def _():
        dp[TT : TT + 8, :] = dp[0:8, :]

    @pl.when(step == count - 1)
    def _():
        ext[0:8, :] = edge_ref[...]

    @pl.when(step < count - 1)
    def _():
        ext[0:8, :] = halo_ref[...].astype(f32)[8:16, :]

    def through_silu(grad, r, at):
        v = pre_ref[r, at].astype(f32)
        gate = sigmoid(v)
        dp[r, at] = grad * (gate * (1.0 + v * (1.0 - gate)))

    strict = (iota2((Q, Q), 0) > iota2((Q, Q), 1)).astype(f32)
    suffix = (iota2((Q, Q), 0) <= iota2((Q, Q), 1)).astype(f32)
    rate = pv_ref[1:2, :]
    for s in reversed(range(SUB)):
        r = slice(s * Q, (s + 1) * Q)
        cum = cum_ref[r, :]
        dt = dt_ref[r, :]
        last = cum[Q - 1 : Q, :]
        tail = jnp.exp2(last - cum) * tok_ref[r, 7:8]
        head = jnp.exp2(cum) * tok_ref[r, 6:7]
        carried = head[Q - 1 : Q, :]
        wide = halves(
            jnp.concatenate([tail, head, dt, jnp.broadcast_to(carried, (16, 128))], axis=0)
        )
        b_in = bc_ref[r, :N]
        c_out = bc_ref[r, N:]
        grad_b = dbc_ref[r, :N]
        grad_c = dbc_ref[r, N:]
        sums = jnp.zeros((3 * Q + 16, 128), f32)
        for b in range(E // W):
            at = slice(b * W, (b + 1) * W)
            grown = nn(wide, e2_ref[:, at])
            dt_wide = grown[2 * Q : 3 * Q]
            after = state[:, at]
            after_low = after.astype(bf16)
            before = prior_ref[s, :, at]
            xs = x_ref[r, at].astype(f32)
            dy = dy_ref[r, at].astype(f32)
            reach = nn(b_in, after_low) * grown[:Q]
            read = nn(c_out, before)
            dxdt = dxdt_ref[r, at].astype(f32) + reach
            dyg = dy * grown[Q : 2 * Q]
            dyg_low = dyg.astype(bf16)
            joint = jnp.sum(after * before.astype(f32), axis=0, keepdims=True)
            stacked = jnp.concatenate(
                [
                    (xs * dxdt).astype(bf16),
                    (xs * reach).astype(bf16),
                    (dyg * read).astype(bf16),
                    jnp.broadcast_to(joint, (16, W)).astype(bf16),
                ],
                axis=0,
            )
            sums = sums + nn(stacked, et_ref[at, :])
            through_silu(dxdt * dt_wide + skip_ref[0:1, at] * dy, r, at)
            grad_c = grad_c + nt(dyg_low, before)
            grad_b = grad_b + nt((xs * (grown[:Q] * dt_wide)).astype(bf16), after_low)
            state[:, at] = after * grown[3 * Q : 3 * Q + 1] + tn(c_out, dyg_low)
        through_silu(grad_b, r, slice(E, E + N))
        through_silu(grad_c, r, slice(E + N, CV))
        dlog = (
            cross_ref[r, :]
            + nn_exact(strict, sums[Q : 2 * Q] * dt)
            + nn_exact(suffix, sums[2 * Q : 3 * Q])
            + carried * sums[3 * Q : 3 * Q + 1]
        )
        draw = (sums[:Q] - rate * dlog) * sigmoid(dtr_ref[r, :] + pv_ref[0:1, :])
        dxc_ref[r, CV:] = draw.astype(bf16)
        hacc_ref[0:1, :] += jnp.sum(draw, axis=0, keepdims=True)
        hacc_ref[1:2, :] -= rate * jnp.sum(dt * dlog, axis=0, keepdims=True)

    ext[8 : TT + 8, :] = xc_ref[...].astype(f32)
    masks = [tok_ref[:, k : k + 1] for k in range(K - 1)]
    ahead = [tok_ref[:, 3 + k : 4 + k] for k in range(K - 1)]
    for b in range(CV // 128):
        at = slice(b * 128, (b + 1) * 128)
        own = dp[0:TT, at]
        total = cw_ref[K - 1 : K, at] * own
        cacc_ref[K : K + 1, at] += jnp.sum(own, axis=0, keepdims=True)
        cacc_ref[K - 1 : K, at] += jnp.sum(own * ext[8 : TT + 8, at], axis=0, keepdims=True)
        for k in range(K - 1):
            total = total + cw_ref[k : k + 1, at] * (dp[3 - k : 3 - k + TT, at] * ahead[k])
            cacc_ref[k : k + 1, at] += jnp.sum(
                own * (ext[5 + k : 5 + k + TT, at] * masks[k]), axis=0, keepdims=True
            )
        dxc_ref[:, at] = total.astype(bf16)

    @pl.when(step == count - 1)
    def _():
        first_ref[...] = dp[0:8, :]


def across_back(
    x, pre, xc, edge, bc, dy, dxdt, dbc, cross, dt, cum, dtr, tok, prior, last, skip, cw, pv, e2,
    et,
):
    t = x.shape[0]
    n = t // TT

    def turned(width):
        return pl.BlockSpec((TT, width), lambda i: (n - 1 - i, 0))

    halo = pl.BlockSpec((16, CV), lambda i: (jnp.maximum((n - 1 - i) * (TT // 16) - 1, 0), 0))
    return pl.pallas_call(
        across_back_kernel,
        grid=(n,),
        in_specs=[
            turned(E), turned(CV), turned(CV), halo, full((8, CV)), turned(2 * N), turned(E),
            turned(E), turned(2 * N), turned(128), turned(128), turned(128), turned(128),
            turned(128), pl.BlockSpec((SUB, N, E), lambda i: (n - 1 - i, 0, 0)), full((N, E)),
            full((1, E)), full((8, CV)), full((8, 128)), full((256, E)), full((E, 128)),
        ],
        out_specs=[turned(CX), full((8, CV)), full((8, 128)), full((8, CV))],
        out_shape=[
            shape((t, CX), bf16),
            shape((8, CV), f32),
            shape((8, 128), f32),
            shape((8, CV), f32),
        ],
        scratch_shapes=[
            pltpu.VMEM((N, E), f32),
            pltpu.VMEM((TT + 8, CV), f32),
            pltpu.VMEM((TT + 8, CV), f32),
        ],
        compiler_params=params(),
        name="across_back",
    )(
        x, pre, xc, xc, edge, bc, dy, dxdt, dbc, cross, dt, cum, dtr, tok, prior, last, skip, cw,
        pv, e2, et,
    )


def close_back_kernel(
    dz_ref, dxc_ref, wz_ref, wx_ref, x_ref, gain_ref, g_ref, new_ref, acc_ref
):
    @pl.when(pl.program_id(0) == 0)
    def _():
        acc_ref[...] = jnp.zeros_like(acc_ref)

    dn = nt(dz_ref[...], wz_ref[...]) + nt(dxc_ref[...], wx_ref[...])
    x = x_ref[...].astype(f32)
    scale = lax.rsqrt(jnp.mean(x * x, axis=-1, keepdims=True) + eps)
    acc_ref[0:1, :] += jnp.sum(dn * (x * scale), axis=0, keepdims=True)
    pulled = dn * gain_ref[...]
    mean = jnp.mean(pulled * x, axis=-1, keepdims=True)
    new_ref[...] = g_ref[...].astype(f32) + scale * pulled - x * (scale * scale * scale * mean)


def close_back(dz, dxc, wz, wx, x, gain, g):
    t = x.shape[0]
    return pl.pallas_call(
        close_back_kernel,
        grid=(t // TT,),
        in_specs=[
            rows(E), rows(CX), full((D, E)), full((D, CX)), rows(D), full((1, D)), rows(D),
        ],
        out_specs=[rows(D), full((8, D))],
        out_shape=[shape((t, D), f32), shape((8, D), f32)],
        compiler_params=params(),
        name="close_back",
    )(dz, dxc, wz, wx, x, gain, g)


def passed_along(value, axis, steps):
    count = lax.axis_size(axis)
    first, last = (max(0, -steps), min(count, count - steps))
    return lax.ppermute(value, axis, [(source, source + steps) for source in range(first, last)])


def swapped(value, axis, bit):
    count = lax.axis_size(axis)
    return lax.ppermute(value, axis, [(source, source ^ bit) for source in range(count)])


def bits_of(axis):
    return [1 << k for k in range((lax.axis_size(axis) - 1).bit_length())]


def all_states(packed):
    bits = bits_of("seq")
    half = E // 2
    sides = [(packed[:, :half], bits[1:] + bits[:1]), (packed[:, half:], bits[:0:-1] + bits[:1])]
    held = [value[None] for value, _ in sides]
    orders = [[0], [0]]
    for k in range(len(bits)):
        for side, (_, path) in enumerate(sides):
            came = swapped(held[side], "seq", path[k])
            held[side] = jnp.concatenate([held[side], came])
            orders[side] = orders[side] + [o ^ path[k] for o in orders[side]]
    return held, orders


def decay_table(held, order):
    logs = held[:, N, :384].astype(f32).reshape(-1, 3, 128).sum(axis=1)
    count = logs.shape[0]
    place = [order.index(k) for k in range(count)]
    return jnp.stack([logs[i] for i in place])


def joined_states(held, orders, logs, forward):
    count, mine = logs.shape[0], lax.axis_index("seq")
    who = jnp.arange(count) ^ mine
    if forward:
        counts = who < mine
        between = (who[None] > who[:, None]) & (who[None] < mine)
    else:
        counts = who > mine
        between = (who[None] < who[:, None]) & (who[None] > mine)
    power = jnp.sum(jnp.where(between[:, :, None], logs[None], 0.0), axis=1)
    factor = jnp.where(counts[:, None], jnp.exp2(power), 0.0)
    factor = jnp.repeat(factor[:, :H], P_SIZE, axis=1)
    half = E // 2
    sides = []
    for side in range(2):
        total = 0.0
        for i, k in enumerate(orders[side]):
            weight = factor[k, side * half : (side + 1) * half]
            total = total + weight[None] * held[side][i, :N].astype(f32)
        sides.append(total)
    return jnp.concatenate(sides, axis=1)


def gathered(piece):
    seqs, parts = lax.axis_size("seq"), lax.axis_size("fsdp")
    height, width = piece.shape
    mine = height // seqs
    own = lax.dynamic_slice_in_dim(piece, lax.axis_index("seq") * mine, mine, 0)
    pieces = lax.all_gather(own, ("seq", "fsdp"))
    pieces = pieces.reshape(seqs, parts, mine, width).transpose(1, 0, 2, 3)
    return pieces.reshape(parts * height, width)


def reduced(value):
    seqs, parts = lax.axis_size("seq"), lax.axis_size("fsdp")
    height, width = value.shape
    value = value.astype(bf16).reshape(parts, height // parts, width)
    value = lax.psum_scatter(value, "seq", scatter_dimension=1, tiled=True)
    value = lax.psum_scatter(value, "fsdp", scatter_dimension=0, tiled=True)
    value = lax.all_gather(value, "seq", axis=1, tiled=True)
    return value[0].astype(f32)


def reduced_small(value):
    parts, mine = lax.axis_size("fsdp"), lax.axis_index("fsdp")
    bit = parts // 2
    while bit:
        value = value.reshape((2, value.shape[0] // 2) + value.shape[1:])
        upper = (mine & bit) != 0
        kept = jnp.where(upper, value[1], value[0])
        value = kept + swapped(jnp.where(upper, value[0], value[1]), "fsdp", bit)
        bit //= 2
    for bit in bits_of("seq"):
        value = value + swapped(value, "seq", bit)
    return value[0]


def pad_lanes(value):
    return jnp.pad(value, ((0, 0), (0, 128 - value.shape[1])))


def token_table(doc, edge_ids):
    t = doc.shape[0]
    widened = jnp.concatenate([edge_ids, doc, jnp.full((K - 1,), -1, doc.dtype)])
    ids = [widened[k : k + t] == doc for k in range(K - 1)]
    ids += [widened[K - 1 + (K - 1 - k) :][:t] == doc for k in range(K - 1)]
    before = widened[K - 2 : K - 2 + t].reshape(t // Q, Q)[:, :1]
    blocks = doc.reshape(t // Q, Q)
    ids.append((blocks == before).reshape(t))
    ids.append((blocks == blocks[:, Q - 1 :]).reshape(t))
    cols_in = [v.astype(f32) for v in ids] + [doc.astype(f32)]
    table = pad_lanes(jnp.stack(cols_in, axis=1))
    return table, jnp.broadcast_to(doc.astype(f32)[None], (8, t))


def constants():
    spread = np.zeros((128, E), np.float32)
    for h in range(H):
        spread[h, h * P_SIZE : (h + 1) * P_SIZE] = 1
    hot = np.zeros((PAIRS, 2 * Q, 128), np.float32)
    sel = np.zeros((PAIRS, HP, 2 * Q), np.float32)
    for p in range(PAIRS):
        for i in range(2):
            hot[p, i * Q : (i + 1) * Q, 2 * p + i] = 1
            sel[p, 2 * p + i, i * Q : (i + 1) * Q] = 1
    return tuple(
        jnp.asarray(v, bf16) for v in (np.concatenate([spread, spread]), spread.T, hot, sel)
    )


SMALL = (K * CV, CV, H, H, H, D, E)


def local(
    first_tier_source,
    token_articles,
    extra_spikes,
    upstream_gradient,
    entering_projection,
    exit_projection,
    filter_kernels,
    filter_shifts,
    stride_shifts,
    log_shrink_rates,
    bypass_coefficient,
    entry_scaling_gains,
    gated_scaling_gains,
):
    current = first_tier_source[0]
    doc = token_articles[0]
    spike = pad_lanes(extra_spikes[0])
    t = doc.shape[0]
    layers = entering_projection.shape[0]
    parts = lax.axis_size("fsdp")
    e2, et, hot, sel = constants()
    edge_ids = passed_along(doc[t - (K - 1) :], "seq", 1)
    tok, doct = token_table(doc, edge_ids)

    small = (
        filter_kernels, filter_shifts, stride_shifts, log_shrink_rates, bypass_coefficient,
        entry_scaling_gains, gated_scaling_gains,
    )
    flat = jnp.concatenate([v.reshape(layers, -1) for v in small], axis=1)
    flat = lax.all_gather(flat, "fsdp").astype(f32)

    def small_of(layer):
        found, at = [], 0
        for size in SMALL:
            width = size // parts
            found.append(flat[:, layer, at : at + width])
            at += width
        taps = found[0].reshape(parts, K, CV // parts).transpose(1, 0, 2).reshape(K, CV)
        return [taps] + [v.reshape(-1) for v in found[1:]]

    weights = [
        (
            gathered(jnp.pad(entering_projection[i][:, E:], ((0, 0), (0, 128 - H)))),
            gathered(entering_projection[i][:, :E]),
            gathered(exit_projection[i]),
        )
        for i in range(layers)
    ]
    kept = []
    for i in range(layers):
        wx, wz, w_out = weights[i]
        taps, shifts, strides, rates, bypass, gain_in, gain_out = small_of(i)
        cw = jnp.concatenate([taps, shifts[None], jnp.zeros((3, CV), f32)])
        pv = jnp.concatenate(
            [pad_lanes(jnp.stack([strides, jnp.exp(rates)])), jnp.zeros((6, 128), f32)]
        )
        skip = jnp.repeat(bypass, P_SIZE)[None]
        gain_in, gain_out = gain_in[None], gain_out[None]
        normed, xc, dtr = project(current, gain_in, wx)
        edge = passed_along(xc[t - (K - 1) :], "seq", 1).astype(f32)
        edge = jnp.concatenate([jnp.zeros((8 - (K - 1), CV), f32), edge])
        pre, x, bc, dt, cum, cumt, dtt, packed = prepare(xc, edge, cw, dtr, spike, tok, pv, e2)
        held, orders = all_states(packed)
        yi = within(x, bc, cum, cumt, dtt, tok, doct)
        z = project_gate(normed, wz)
        logs = decay_table(held[0], orders[0])
        incoming = joined_states(held, orders, logs, True)
        out_type = bf16 if i == layers - 1 else f32
        y, low, new, prior = across(
            yi, x, bc, dt, cum, tok, z, incoming, skip, gain_out, w_out, current, e2, out_type
        )
        kept.append(
            (current, normed, z, xc, dtr, edge, pre, x, bc, dt, cum, cumt, logs, y, low, prior,
             cw, pv, skip, gain_in, gain_out)
        )
        current = new
    grad = upstream_gradient[0]
    results = [None] * layers
    for i in reversed(range(layers)):
        wx, wz, w_out = weights[i]
        (source, normed, z, xc, dtr, edge, pre, x, bc, dt, cum, cumt, logs, y, low, prior,
         cw, pv, skip, gain_in, gain_out) = kept[i]
        dy, dz, gb, acc, state = open_back(
            grad, w_out, y, z, x, bc, cum, tok, gain_out, e2
        )
        held, orders = all_states(state)
        grad_out = reduced(tn(low, gb))
        grad_gate = reduced(tn(normed, dz))
        dxdt, dbc, cross = within_back(x, dy, bc, dt, cum, cumt, tok, doct, hot, sel)
        later = joined_states(held, orders, logs, False)
        dxc, cacc, hacc, first = across_back(
            x, pre, xc, edge, bc, dy, dxdt, dbc, cross, dt, cum, dtr, tok, prior, later, skip, cw,
            pv, e2, et,
        )
        masked = [first[: K - 1] * tok[: K - 1, k : k + 1] for k in range(K - 1)]
        borrowed = jnp.stack(
            [sum(cw[k] * masked[k][e - k] for k in range(e + 1)) for e in range(K - 1)]
        )
        back = passed_along(borrowed, "seq", -1)
        mended = (dxc[t - (K - 1) :, :CV].astype(f32) + back).astype(bf16)
        dxc = dxc.at[t - (K - 1) :, :CV].set(mended)
        grad_conv = reduced(tn(normed, dxc))
        grad, nacc = close_back(dz, dxc, wz, wx, source, gain_in, grad)
        big = (jnp.concatenate([grad_gate, grad_conv[:, : CV + H]], axis=1), grad_out)
        tiny = [
            cacc[:K], cacc[K], hacc[0, :H], hacc[1, :H],
            jnp.sum(acc[1].reshape(H, P_SIZE), axis=1), nacc[0], acc[0],
        ]
        results[i] = (big, tiny)
    packed = []
    for i in range(layers):
        tiny = results[i][1]
        taps = tiny[0].reshape(K, parts, CV // parts).transpose(1, 0, 2).reshape(parts, -1)
        packed.append(jnp.concatenate([taps] + [v.reshape(parts, -1) for v in tiny[1:]], axis=1))
    mine = reduced_small(jnp.stack(packed, axis=1))
    smalls, at = [], 0
    for size in SMALL:
        width = size // parts
        smalls.append(mine[:, at : at + width])
        at += width
    smalls[0] = smalls[0].reshape(layers, K, CV // parts)
    bigs = [jnp.stack([results[i][0][j] for i in range(layers)]) for j in range(2)]
    return (current[None], grad[None], *bigs, *smalls)


def solution(mesh):
    placed = (
        P("fsdp", "seq", None),
        P("fsdp", "seq"),
        P("fsdp", "seq", None),
        P("fsdp", "seq", None),
        P(None, "fsdp", None),
        P(None, "fsdp", None),
        P(None, None, "fsdp"),
        P(None, "fsdp"),
        P(None, "fsdp"),
        P(None, "fsdp"),
        P(None, "fsdp"),
        P(None, "fsdp"),
        P(None, "fsdp"),
    )
    return jax.shard_map(
        local,
        mesh=mesh,
        in_specs=placed,
        out_specs=(
            P("fsdp", "seq", None),
            P("fsdp", "seq", None),
            P(None, "fsdp", None),
            P(None, "fsdp", None),
            P(None, None, "fsdp"),
            P(None, "fsdp"),
            P(None, "fsdp"),
            P(None, "fsdp"),
            P(None, "fsdp"),
            P(None, "fsdp"),
            P(None, "fsdp"),
        ),
        check_vma=False,
    )
```

```python
from functools import partial

import jax
import jax.numpy as jnp
import numpy as np
from jax import lax
from jax.experimental import pallas as pl
from jax.experimental.pallas import tpu as pltpu
from jax.sharding import PartitionSpec as P

D = 768
H = 24
P_SIZE = 64
N = 128
K = 4
E = 1536
CV = 1792
HX = CV // 2
HZ = E // 2
HD = D // 2
CX = HX + 128
Q = 128
TT = 256
SUB = TT // Q
W = 256
HP = 32
PAIRS = H // 2
eps = 1e-05
LOG2E = 1.4426950408889634
BIG = -1e30
CUT = 30000.0
f32 = jnp.float32
bf16 = jnp.bfloat16
highest = lax.Precision.HIGHEST
VMEM_LIMIT = 56 * 1024 * 1024


def nn(a, b):
    return lax.dot_general(a, b, (((1,), (0,)), ((), ())), preferred_element_type=f32)


def nt(a, b):
    return lax.dot_general(a, b, (((1,), (1,)), ((), ())), preferred_element_type=f32)


def tn(a, b):
    return lax.dot_general(a, b, (((0,), (0,)), ((), ())), preferred_element_type=f32)


def nn_exact(a, b):
    return lax.dot_general(
        a, b, (((1,), (0,)), ((), ())), precision=highest, preferred_element_type=f32
    )


def halves(v):
    hi = v.astype(bf16)
    lo = (v - hi.astype(f32)).astype(bf16)
    return jnp.concatenate([hi, lo], axis=1)


def sigmoid(v):
    return 0.5 + 0.5 * jnp.tanh(0.5 * v)


def softplus(v):
    return jnp.maximum(v, 0.0) + jnp.log1p(jnp.exp(-jnp.abs(v)))


def iota2(shape, dim):
    return lax.broadcasted_iota(jnp.int32, shape, dim)


def lane_halves():
    lane = iota2((1, 2 * P_SIZE), 1)
    left = (lane < P_SIZE).astype(f32).astype(bf16)
    right = (lane >= P_SIZE).astype(f32).astype(bf16)
    return left, right


def full(shape):
    return pl.BlockSpec(shape, lambda i: (0,) * len(shape))


def rows(width, size=TT):
    return pl.BlockSpec((size, width), lambda i: (i, 0))


def cols(height):
    return pl.BlockSpec((height, TT), lambda i: (0, i))


def params():
    return pltpu.CompilerParams(vmem_limit_bytes=VMEM_LIMIT, dimension_semantics=("arbitrary",))


def cost(micros):
    return pl.CostEstimate(
        flops=int(micros * 1e9), bytes_accessed=int(micros * 3e6), transcendentals=0
    )


SMEM = pl.BlockSpec(memory_space=pltpu.SMEM)


def sides(core_ref, width):
    mine = core_ref[0] * width
    return pl.ds(pl.multiple_of(mine, 128), width), pl.ds(
        pl.multiple_of(width - mine, 128), width
    )


def shape(dims, dtype):
    return jax.ShapeDtypeStruct(dims, dtype)


def project_kernel(core_ref, x_ref, gain_ref, mine_ref, other_ref, normed_ref, xc_ref, dtr_ref):
    x = x_ref[...].astype(f32)
    scale = lax.rsqrt(jnp.mean(x * x, axis=-1, keepdims=True) + eps)
    normed = (x * scale * gain_ref[...]).astype(bf16)
    normed_ref[...] = normed
    own, far = sides(core_ref, HX)
    xc_ref[:, own] = nn(normed, mine_ref[:, :HX]).astype(bf16)
    dtr_ref[...] = nn(normed, mine_ref[:, HX:])
    xc_ref[:, far] = nn(normed, other_ref[:, :HX]).astype(bf16)


def project(core, x, gain, mine, other):
    t = x.shape[0]
    return pl.pallas_call(
        project_kernel,
        grid=(t // TT,),
        in_specs=[SMEM, rows(D), full((1, D)), full((D, CX)), full((D, CX))],
        out_specs=[rows(D), rows(CV), rows(128)],
        out_shape=[shape((t, D), bf16), shape((t, CV), bf16), shape((t, 128), f32)],
        compiler_params=params(),
        cost_estimate=cost(8),
        name="project",
    )(core, x, gain, mine, other)


def gate_kernel(core_ref, normed_ref, mine_ref, other_ref, z_ref):
    own, far = sides(core_ref, HZ)
    z_ref[:, own] = nn(normed_ref[...], mine_ref[...]).astype(bf16)
    z_ref[:, far] = nn(normed_ref[...], other_ref[...]).astype(bf16)


def project_gate(core, normed, mine, other):
    t = normed.shape[0]
    return pl.pallas_call(
        gate_kernel,
        grid=(t // TT,),
        in_specs=[SMEM, rows(D), full((D, HZ)), full((D, HZ))],
        out_specs=rows(E),
        out_shape=shape((t, E), bf16),
        compiler_params=params(),
        cost_estimate=cost(6),
        name="project_gate",
    )(core, normed, mine, other)


def prepare_kernel(
    xc_ref, edge_ref, cw_ref, dtr_ref, spike_ref, tok_ref, pv_ref, e2_ref,
    pre_ref, x_ref, bc_ref, dt_ref, cum_ref, cumt_ref, dtt_ref, packed_ref,
    ext, state_ref, carry_ref,
):
    step = pl.program_id(0)

    @pl.when(step == 0)
    def _():
        ext[0:8, :] = edge_ref[...]
        state_ref[...] = jnp.zeros_like(state_ref)
        carry_ref[...] = jnp.zeros_like(carry_ref)

    @pl.when(step > 0)
    def _():
        ext[0:8, :] = ext[TT : TT + 8, :]

    ext[8 : TT + 8, :] = xc_ref[...].astype(f32)
    masks = [tok_ref[:, k : k + 1] for k in range(K - 1)]
    for b in range(CV // 128):
        at = slice(b * 128, (b + 1) * 128)
        total = cw_ref[K : K + 1, at] + cw_ref[K - 1 : K, at] * ext[8 : TT + 8, at]
        for k in range(K - 1):
            total = total + cw_ref[k : k + 1, at] * (ext[5 + k : 5 + k + TT, at] * masks[k])
        pre_ref[:, at] = total.astype(bf16)
        act = (total * sigmoid(total)).astype(bf16)
        if b < E // 128:
            x_ref[:, at] = act
        else:
            bc_ref[:, (b - E // 128) * 128 : (b - E // 128 + 1) * 128] = act

    dt = softplus(dtr_ref[...] + pv_ref[0:1, :])
    log_decay = (spike_ref[...] - dt * pv_ref[1:2, :]) * LOG2E
    dt_ref[...] = dt
    dtt_ref[...] = jnp.transpose(dt)[:HP, :]
    lower = (iota2((Q, Q), 0) >= iota2((Q, Q), 1)).astype(f32)
    for s in range(SUB):
        r = slice(s * Q, (s + 1) * Q)
        cum = nn_exact(lower, log_decay[r])
        cum_ref[r, :] = cum
        cumt_ref[:, r] = jnp.transpose(cum)[:HP, :]
        last = cum[Q - 1 : Q, :]
        tail = jnp.exp2(last - cum) * tok_ref[r, 7:8] * dt[r]
        kept = tok_ref[s * Q + Q - 1 : s * Q + Q, 6:7]
        carried = jnp.exp2(last) * kept
        carry_ref[...] = carry_ref[...] + (last + (kept - 1.0) * CUT)
        wide = jnp.concatenate([tail, jnp.broadcast_to(carried, (16, 128))], axis=0)
        wide = halves(wide)
        b_in = bc_ref[r, :N]
        for b in range(E // W):
            at = slice(b * W, (b + 1) * W)
            grown = nn(wide, e2_ref[:, at])
            weighted = (x_ref[r, at].astype(f32) * grown[:Q]).astype(bf16)
            state_ref[:, at] = state_ref[:, at] * grown[Q : Q + 1] + tn(b_in, weighted)

    @pl.when(step == pl.num_programs(0) - 1)
    def _():
        packed_ref[:N, :] = state_ref[...].astype(bf16)
        packed_ref[N:, :] = jnp.zeros((16, E), bf16)
        rest = jnp.concatenate([carry_ref[...], carry_ref[...]], axis=0)
        for k in range(3):
            part = rest.astype(bf16)
            packed_ref[N:, k * 128 : (k + 1) * 128] = part
            rest = rest - part.astype(f32)


def prepare(xc, edge, cw, dtr, spike, tok, pv, e2):
    t = xc.shape[0]
    return pl.pallas_call(
        prepare_kernel,
        grid=(t // TT,),
        in_specs=[
            rows(CV), full((8, CV)), full((8, CV)), rows(128), rows(128), rows(128),
            full((8, 128)), full((256, E)),
        ],
        out_specs=[
            rows(CV), rows(E), rows(2 * N), rows(128), rows(128), cols(HP), cols(HP),
            full((N + 16, E)),
        ],
        out_shape=[
            shape((t, CV), bf16),
            shape((t, E), bf16),
            shape((t, 2 * N), bf16),
            shape((t, 128), f32),
            shape((t, 128), f32),
            shape((HP, t), f32),
            shape((HP, t), f32),
            shape((N + 16, E), bf16),
        ],
        scratch_shapes=[
            pltpu.VMEM((TT + 8, CV), f32),
            pltpu.VMEM((N, E), f32),
            pltpu.VMEM((8, 128), f32),
        ],
        compiler_params=params(),
        cost_estimate=cost(15),
        name="prepare",
    )(xc, edge, cw, dtr, spike, tok, pv, e2)


def within_kernel(x_ref, bc_ref, cum_ref, cumt_ref, dtt_ref, tok_ref, doct_ref, y_ref):
    left, right = lane_halves()
    order = iota2((Q, Q), 0) >= iota2((Q, Q), 1)
    for s in range(SUB):
        r = slice(s * Q, (s + 1) * Q)
        same = tok_ref[r, 8:9] == doct_ref[0:1, r]
        bias = jnp.where(order & same, 0.0, BIG)
        scores = nt(bc_ref[r, N:], bc_ref[r, :N])
        cum = cum_ref[r, :]
        for p in range(PAIRS):
            at = slice(p * 128, (p + 1) * 128)
            xp = x_ref[r, at]
            mixes = []
            for h in (2 * p, 2 * p + 1):
                gap = (cum[:, h : h + 1] - cumt_ref[h : h + 1, r]) + bias
                mixes.append((jnp.exp2(gap) * (scores * dtt_ref[h : h + 1, r])).astype(bf16))
            both = jnp.concatenate([xp * left, xp * right], axis=0)
            y_ref[r, at] = nn(jnp.concatenate(mixes, axis=1), both).astype(bf16)


def within(x, bc, cum, cumt, dtt, tok, doct):
    t = x.shape[0]
    return pl.pallas_call(
        within_kernel,
        grid=(t // TT,),
        in_specs=[rows(E), rows(2 * N), rows(128), cols(HP), cols(HP), rows(128), cols(8)],
        out_specs=rows(E),
        out_shape=shape((t, E), bf16),
        compiler_params=params(),
        cost_estimate=cost(8),
        name="within",
    )(x, bc, cum, cumt, dtt, tok, doct)


def across_kernel(
    core_ref, yi_ref, x_ref, bc_ref, dt_ref, cum_ref, tok_ref, z_ref, first_ref, skip_ref,
    gain_ref, mine_ref, other_ref, res_ref, e2_ref,
    y_ref, low_ref, new_ref, prior_ref,
    state, gated,
):
    step = pl.program_id(0)

    @pl.when(step == 0)
    def _():
        state[...] = first_ref[...]

    for s in range(SUB):
        r = slice(s * Q, (s + 1) * Q)
        cum = cum_ref[r, :]
        last = cum[Q - 1 : Q, :]
        tail = jnp.exp2(last - cum) * tok_ref[r, 7:8] * dt_ref[r, :]
        head = jnp.exp2(cum) * tok_ref[r, 6:7]
        carried = head[Q - 1 : Q, :]
        wide = halves(
            jnp.concatenate([tail, head, jnp.broadcast_to(carried, (16, 128))], axis=0)
        )
        b_in = bc_ref[r, :N]
        c_out = bc_ref[r, N:]
        square = jnp.zeros((Q, W), f32)
        for b in range(E // W):
            at = slice(b * W, (b + 1) * W)
            grown = nn(wide, e2_ref[:, at])
            xs = x_ref[r, at].astype(f32)
            held = state[:, at]
            prior_ref[s, :, at] = held.astype(bf16)
            y = (
                yi_ref[r, at].astype(f32)
                + nn(c_out, held.astype(bf16)) * grown[Q : 2 * Q]
                + skip_ref[0:1, at] * xs
            )
            y_ref[r, at] = y.astype(bf16)
            z = z_ref[r, at].astype(f32)
            made = y * (z * sigmoid(z))
            gated[r, at] = made
            square = square + made * made
            weighted = (xs * grown[:Q]).astype(bf16)
            state[:, at] = held * grown[2 * Q : 2 * Q + 1] + tn(b_in, weighted)
        scale = lax.rsqrt(jnp.sum(square, axis=-1, keepdims=True) * (1.0 / E) + eps)
        for b in range(E // W):
            at = slice(b * W, (b + 1) * W)
            low_ref[r, at] = (gated[r, at] * scale * gain_ref[0:1, at]).astype(bf16)
    for at, w_ref in zip(sides(core_ref, HD), (mine_ref, other_ref)):
        new = res_ref[:, at].astype(f32) + nn(low_ref[...], w_ref[...])
        new_ref[:, at] = new.astype(new_ref.dtype)


def across(core, yi, x, bc, dt, cum, tok, z, first, skip, gain, mine, other, res, e2, out_type):
    t = x.shape[0]
    return pl.pallas_call(
        across_kernel,
        grid=(t // TT,),
        in_specs=[
            SMEM, rows(E), rows(E), rows(2 * N), rows(128), rows(128), rows(128), rows(E),
            full((N, E)), full((1, E)), full((1, E)), full((E, HD)), full((E, HD)), rows(D),
            full((256, E)),
        ],
        out_specs=[rows(E), rows(E), rows(D), pl.BlockSpec((SUB, N, E), lambda i: (i, 0, 0))],
        out_shape=[
            shape((t, E), bf16),
            shape((t, E), bf16),
            shape((t, D), out_type),
            shape((t // Q, N, E), bf16),
        ],
        scratch_shapes=[pltpu.VMEM((N, E), f32), pltpu.VMEM((TT, E), f32)],
        compiler_params=params(),
        cost_estimate=cost(16),
        name="across",
    )(core, yi, x, bc, dt, cum, tok, z, first, skip, gain, mine, other, res, e2)


def open_back_kernel(
    core_ref, g_ref, mine_ref, other_ref, y_ref, z_ref, x_ref, bc_ref, cum_ref, tok_ref,
    gain_ref, e2_ref,
    dy_ref, dz_ref, gb_ref, acc_ref, low_ref,
    held, state_ref,
):
    step = pl.program_id(0)

    @pl.when(step == 0)
    def _():
        acc_ref[...] = jnp.zeros_like(acc_ref)
        state_ref[...] = jnp.zeros_like(state_ref)

    gb_ref[...] = g_ref[...].astype(bf16)
    own, far = sides(core_ref, HD)
    held[...] = nt(gb_ref[:, own], mine_ref[...]) + nt(gb_ref[:, far], other_ref[...])
    for s in reversed(range(SUB)):
        r = slice(s * Q, (s + 1) * Q)
        square = jnp.zeros((Q, W), f32)
        cross = jnp.zeros((Q, W), f32)
        for b in range(E // W):
            at = slice(b * W, (b + 1) * W)
            z = z_ref[r, at].astype(f32)
            gated = y_ref[r, at].astype(f32) * (z * sigmoid(z))
            square = square + gated * gated
            cross = cross + gated * (held[r, at] * gain_ref[0:1, at])
        scale = lax.rsqrt(jnp.sum(square, axis=-1, keepdims=True) * (1.0 / E) + eps)
        pull = (scale * scale * scale) * (jnp.sum(cross, axis=-1, keepdims=True) * (1.0 / E))
        cum = cum_ref[r, :]
        head = jnp.exp2(cum) * tok_ref[r, 6:7]
        wide = halves(
            jnp.concatenate([head, jnp.broadcast_to(head[Q - 1 : Q, :], (16, 128))], axis=0)
        )
        c_out = bc_ref[r, N:]
        for b in range(E // W):
            at = slice(b * W, (b + 1) * W)
            z = z_ref[r, at].astype(f32)
            gate = sigmoid(z)
            y = y_ref[r, at].astype(f32)
            gated = y * (z * gate)
            dn = held[r, at]
            acc_ref[0:1, at] += jnp.sum(dn * (gated * scale), axis=0, keepdims=True)
            dgated = scale * (dn * gain_ref[0:1, at]) - gated * pull
            dy = dgated * (z * gate)
            dz_ref[r, at] = (dgated * y * (gate * (1.0 + z * (1.0 - gate)))).astype(bf16)
            acc_ref[1:2, at] += jnp.sum(dy * x_ref[r, at].astype(f32), axis=0, keepdims=True)
            dy_ref[r, at] = dy.astype(bf16)
            grown = nn(wide, e2_ref[:, at])
            state_ref[:, at] = state_ref[:, at] * grown[Q : Q + 1] + tn(
                c_out, (dy * grown[:Q]).astype(bf16)
            )

    @pl.when(step == pl.num_programs(0) - 1)
    def _():
        low_ref[...] = state_ref[...].astype(bf16)


def open_back(core, g, mine, other, y, z, x, bc, cum, tok, gain, e2):
    t = x.shape[0]
    n = t // TT

    def turned(width):
        return pl.BlockSpec((TT, width), lambda i: (n - 1 - i, 0))

    return pl.pallas_call(
        open_back_kernel,
        grid=(n,),
        in_specs=[
            SMEM, turned(D), full((E, HD)), full((E, HD)), turned(E), turned(E), turned(E),
            turned(2 * N), turned(128), turned(128), full((1, E)), full((256, E)),
        ],
        out_specs=[turned(E), turned(E), turned(D), full((8, E)), full((N, E))],
        out_shape=[
            shape((t, E), bf16),
            shape((t, E), bf16),
            shape((t, D), bf16),
            shape((8, E), f32),
            shape((N, E), bf16),
        ],
        scratch_shapes=[pltpu.VMEM((TT, E), f32), pltpu.VMEM((N, E), f32)],
        compiler_params=params(),
        cost_estimate=cost(20),
        name="open_back",
    )(core, g, mine, other, y, z, x, bc, cum, tok, gain, e2)


def within_back_kernel(
    pairs,
    x_ref, dy_ref, bc_ref, dt_ref, cum_ref, cumt_ref, tok_ref, doct_ref, hot_ref, sel_ref,
    dxdt_ref, dbc_ref, cross_ref,
):
    left, right = lane_halves()
    order = iota2((Q, Q), 1) >= iota2((Q, Q), 0)
    suffix = order.astype(f32)
    for s in range(SUB):
        r = slice(s * Q, (s + 1) * Q)
        same = tok_ref[r, 8:9] == doct_ref[0:1, r]
        bias = jnp.where(order & same, 0.0, BIG)
        b_in = bc_ref[r, :N]
        c_out = bc_ref[r, N:]
        scores = nt(b_in, c_out)
        cum = cum_ref[r, :]
        dt = dt_ref[r, :]
        grad_scores = jnp.zeros((Q, Q), f32)
        by_source = jnp.zeros((Q, 128), f32)
        by_target = jnp.zeros((HP, Q), f32)
        for p in pairs:
            at = slice((p - pairs[0]) * 128, (p - pairs[0] + 1) * 128)
            xp = x_ref[r, at]
            dyp = dy_ref[r, at]
            dmix = nt(jnp.concatenate([xp * left, xp * right], axis=0), dyp)
            mixes = []
            flows = []
            for i in range(2):
                h = 2 * p + i
                decay = jnp.exp2((cumt_ref[h : h + 1, r] - cum[:, h : h + 1]) + bias)
                mixes.append((decay * scores).astype(bf16))
                part = dmix[i * Q : (i + 1) * Q] * (decay * dt[:, h : h + 1])
                grad_scores = grad_scores + part
                flows.append((part * scores).astype(bf16))
            both = jnp.concatenate([dyp * left, dyp * right], axis=0)
            dxdt_ref[r, at] = nn(jnp.concatenate(mixes, axis=1), both).astype(bf16)
            by_source = by_source + nn(
                jnp.concatenate(flows, axis=1), hot_ref[p - pairs[0]]
            )
            by_target = by_target + nn(
                sel_ref[p - pairs[0]], jnp.concatenate(flows, axis=0)
            )
        low = grad_scores.astype(bf16)
        dbc_ref[r, :N] = nn(low, c_out)
        dbc_ref[r, N:] = tn(low, b_in)
        target = jnp.transpose(
            jnp.concatenate([by_target, jnp.zeros((128 - HP, Q), f32)], axis=0)
        )
        cross_ref[r, :] = nn_exact(suffix, target - by_source)


def within_back(x, dy, bc, dt, cum, cumt, tok, doct, hot, sel, part):
    t = x.shape[0]
    size = PAIRS // 2
    half = pl.BlockSpec((TT, HZ), lambda i: (i, part))
    return pl.pallas_call(
        partial(within_back_kernel, range(part * size, (part + 1) * size)),
        grid=(t // TT,),
        in_specs=[
            half, half, rows(2 * N), rows(128), rows(128), cols(HP), rows(128), cols(8),
            pl.BlockSpec((size,) + hot.shape[1:], lambda i: (part, 0, 0)),
            pl.BlockSpec((size,) + sel.shape[1:], lambda i: (part, 0, 0)),
        ],
        out_specs=[rows(HZ), rows(2 * N), rows(128)],
        out_shape=[shape((t, HZ), bf16), shape((t, 2 * N), f32), shape((t, 128), f32)],
        compiler_params=params(),
        cost_estimate=cost(12),
        name="within_back",
    )(x, dy, bc, dt, cum, cumt, tok, doct, hot, sel)


def across_back_kernel(
    x_ref, pre_ref, xc_ref, halo_ref, edge_ref, bc_ref, dy_ref, dxdt0_ref, dxdt1_ref,
    dbc0_ref, dbc1_ref, cross0_ref, cross1_ref,
    dt_ref, cum_ref, dtr_ref, tok_ref, prior_ref, last_ref, skip_ref, cw_ref, pv_ref, e2_ref,
    et_ref,
    dxc_ref, cacc_ref, hacc_ref, first_ref,
    state, dp, ext,
):
    step = pl.program_id(0)
    count = pl.num_programs(0)

    @pl.when(step == 0)
    def _():
        state[...] = last_ref[...]
        cacc_ref[...] = jnp.zeros_like(cacc_ref)
        hacc_ref[...] = jnp.zeros_like(hacc_ref)
        dp[TT : TT + 8, :] = jnp.zeros((8, CV), f32)

    @pl.when(step > 0)
    def _():
        dp[TT : TT + 8, :] = dp[0:8, :]

    @pl.when(step == count - 1)
    def _():
        ext[0:8, :] = edge_ref[...]

    @pl.when(step < count - 1)
    def _():
        ext[0:8, :] = halo_ref[...].astype(f32)[8:16, :]

    def through_silu(grad, r, at):
        v = pre_ref[r, at].astype(f32)
        gate = sigmoid(v)
        dp[r, at] = grad * (gate * (1.0 + v * (1.0 - gate)))

    strict = (iota2((Q, Q), 0) > iota2((Q, Q), 1)).astype(f32)
    suffix = (iota2((Q, Q), 0) <= iota2((Q, Q), 1)).astype(f32)
    rate = pv_ref[1:2, :]
    for s in reversed(range(SUB)):
        r = slice(s * Q, (s + 1) * Q)
        cum = cum_ref[r, :]
        dt = dt_ref[r, :]
        last = cum[Q - 1 : Q, :]
        tail = jnp.exp2(last - cum) * tok_ref[r, 7:8]
        head = jnp.exp2(cum) * tok_ref[r, 6:7]
        carried = head[Q - 1 : Q, :]
        wide = halves(
            jnp.concatenate([tail, head, dt, jnp.broadcast_to(carried, (16, 128))], axis=0)
        )
        b_in = bc_ref[r, :N]
        c_out = bc_ref[r, N:]
        grad_b = dbc0_ref[r, :N] + dbc1_ref[r, :N]
        grad_c = dbc0_ref[r, N:] + dbc1_ref[r, N:]
        sums = jnp.zeros((3 * Q + 16, 128), f32)
        for b in range(E // W):
            at = slice(b * W, (b + 1) * W)
            grown = nn(wide, e2_ref[:, at])
            dt_wide = grown[2 * Q : 3 * Q]
            after = state[:, at]
            after_low = after.astype(bf16)
            before = prior_ref[s, :, at]
            xs = x_ref[r, at].astype(f32)
            dy = dy_ref[r, at].astype(f32)
            reach = nn(b_in, after_low) * grown[:Q]
            read = nn(c_out, before)
            near = (dxdt0_ref, dxdt1_ref)[b * W // HZ]
            dxdt = near[r, b * W % HZ : b * W % HZ + W].astype(f32) + reach
            dyg = dy * grown[Q : 2 * Q]
            dyg_low = dyg.astype(bf16)
            joint = jnp.sum(after * before.astype(f32), axis=0, keepdims=True)
            stacked = jnp.concatenate(
                [
                    (xs * dxdt).astype(bf16),
                    (xs * reach).astype(bf16),
                    (dyg * read).astype(bf16),
                    jnp.broadcast_to(joint, (16, W)).astype(bf16),
                ],
                axis=0,
            )
            sums = sums + nn(stacked, et_ref[at, :])
            through_silu(dxdt * dt_wide + skip_ref[0:1, at] * dy, r, at)
            grad_c = grad_c + nt(dyg_low, before)
            grad_b = grad_b + nt((xs * (grown[:Q] * dt_wide)).astype(bf16), after_low)
            state[:, at] = after * grown[3 * Q : 3 * Q + 1] + tn(c_out, dyg_low)
        through_silu(grad_b, r, slice(E, E + N))
        through_silu(grad_c, r, slice(E + N, CV))
        dlog = (
            cross0_ref[r, :]
            + cross1_ref[r, :]
            + nn_exact(strict, sums[Q : 2 * Q] * dt)
            + nn_exact(suffix, sums[2 * Q : 3 * Q])
            + carried * sums[3 * Q : 3 * Q + 1]
        )
        draw = (sums[:Q] - rate * dlog) * sigmoid(dtr_ref[r, :] + pv_ref[0:1, :])
        dxc_ref[r, HX:CX] = draw.astype(bf16)
        dxc_ref[r, CX + HX :] = draw.astype(bf16)
        hacc_ref[0:1, :] += jnp.sum(draw, axis=0, keepdims=True)
        hacc_ref[1:2, :] -= rate * jnp.sum(dt * dlog, axis=0, keepdims=True)

    ext[8 : TT + 8, :] = xc_ref[...].astype(f32)
    masks = [tok_ref[:, k : k + 1] for k in range(K - 1)]
    ahead = [tok_ref[:, 3 + k : 4 + k] for k in range(K - 1)]
    for b in range(CV // 128):
        at = slice(b * 128, (b + 1) * 128)
        own = dp[0:TT, at]
        total = cw_ref[K - 1 : K, at] * own
        cacc_ref[K : K + 1, at] += jnp.sum(own, axis=0, keepdims=True)
        cacc_ref[K - 1 : K, at] += jnp.sum(own * ext[8 : TT + 8, at], axis=0, keepdims=True)
        for k in range(K - 1):
            total = total + cw_ref[k : k + 1, at] * (dp[3 - k : 3 - k + TT, at] * ahead[k])
            cacc_ref[k : k + 1, at] += jnp.sum(
                own * (ext[5 + k : 5 + k + TT, at] * masks[k]), axis=0, keepdims=True
            )
        to = b * 128 + (128 if b * 128 >= HX else 0)
        dxc_ref[:, to : to + 128] = total.astype(bf16)

    @pl.when(step == count - 1)
    def _():
        first_ref[...] = dp[0:8, :]


def across_back(
    x, pre, xc, edge, bc, dy, near0, near1, dt, cum, dtr, tok, prior, last, skip, cw, pv, e2, et
):
    t = x.shape[0]
    n = t // TT

    def turned(width):
        return pl.BlockSpec((TT, width), lambda i: (n - 1 - i, 0))

    halo = pl.BlockSpec((16, CV), lambda i: (jnp.maximum((n - 1 - i) * (TT // 16) - 1, 0), 0))
    return pl.pallas_call(
        across_back_kernel,
        grid=(n,),
        in_specs=[
            turned(E), turned(CV), turned(CV), halo, full((8, CV)), turned(2 * N), turned(E),
            turned(HZ), turned(HZ), turned(2 * N), turned(2 * N), turned(128), turned(128),
            turned(128), turned(128), turned(128), turned(128), pl.BlockSpec((SUB, N, E), lambda i: (n - 1 - i, 0, 0)), full((N, E)),
            full((1, E)), full((8, CV)), full((8, 128)), full((256, E)), full((E, 128)),
        ],
        out_specs=[turned(2 * CX), full((8, CV)), full((8, 128)), full((8, CV))],
        out_shape=[
            shape((t, 2 * CX), bf16),
            shape((8, CV), f32),
            shape((8, 128), f32),
            shape((8, CV), f32),
        ],
        scratch_shapes=[
            pltpu.VMEM((N, E), f32),
            pltpu.VMEM((TT + 8, CV), f32),
            pltpu.VMEM((TT + 8, CV), f32),
        ],
        compiler_params=params(),
        cost_estimate=cost(31),
        name="across_back",
    )(
        x, pre, xc, xc, edge, bc, dy, near0[0], near1[0], near0[1], near1[1], near0[2], near1[2],
        dt, cum, dtr, tok, prior, last, skip, cw, pv, e2, et,
    )


def close_back_kernel(
    core_ref, dz_ref, dxc_ref, zm_ref, zo_ref, xm_ref, xo_ref, x_ref, gain_ref, g_ref,
    new_ref, acc_ref,
):
    @pl.when(pl.program_id(0) == 0)
    def _():
        acc_ref[...] = jnp.zeros_like(acc_ref)

    own_z, far_z = sides(core_ref, HZ)
    own_x, far_x = sides(core_ref, CX)
    dn = (
        nt(dz_ref[:, own_z], zm_ref[...])
        + nt(dz_ref[:, far_z], zo_ref[...])
        + nt(dxc_ref[:, own_x], xm_ref[...])
        + nt(dxc_ref[:, far_x][:, :HX], xo_ref[:, :HX])
    )
    x = x_ref[...].astype(f32)
    scale = lax.rsqrt(jnp.mean(x * x, axis=-1, keepdims=True) + eps)
    acc_ref[0:1, :] += jnp.sum(dn * (x * scale), axis=0, keepdims=True)
    pulled = dn * gain_ref[...]
    mean = jnp.mean(pulled * x, axis=-1, keepdims=True)
    new_ref[...] = g_ref[...].astype(f32) + scale * pulled - x * (scale * scale * scale * mean)


def close_back(core, dz, dxc, zs, xs, x, gain, g):
    t = x.shape[0]
    return pl.pallas_call(
        close_back_kernel,
        grid=(t // TT,),
        in_specs=[
            SMEM, rows(E), rows(2 * CX), full((D, HZ)), full((D, HZ)), full((D, CX)),
            full((D, CX)), rows(D), full((1, D)), rows(D),
        ],
        out_specs=[rows(D), full((8, D))],
        out_shape=[shape((t, D), f32), shape((8, D), f32)],
        compiler_params=params(),
        cost_estimate=cost(12),
        name="close_back",
    )(core, dz, dxc, *zs, *xs, x, gain, g)


def passed_along(value, axis, steps):
    count = lax.axis_size(axis)
    first, last = (max(0, -steps), min(count, count - steps))
    return lax.ppermute(value, axis, [(source, source + steps) for source in range(first, last)])


def swapped(value, axis, bit):
    count = lax.axis_size(axis)
    return lax.ppermute(value, axis, [(source, source ^ bit) for source in range(count)])


def bits_of(axis):
    return [1 << k for k in range((lax.axis_size(axis) - 1).bit_length())]


def all_states(packed, *beside):
    bits = bits_of("seq")
    half = E // 2
    sides = [(packed[:, :half], bits[1:] + bits[:1]), (packed[:, half:], bits[:0:-1] + bits[:1])]
    held = [value[None] for value, _ in sides]
    orders = [[0], [0]]
    stages = []
    for k in range(len(bits)):
        before = tuple(held)
        for side, (_, path) in enumerate(sides):
            came = swapped(held[side], "seq", path[k])
            held[side] = jnp.concatenate([held[side], came])
            orders[side] = orders[side] + [o ^ path[k] for o in orders[side]]
        fill = [make(before) for make in beside[k : k + 1]]
        held = list(together(*held, *fill))[:2]
        stages.append(tuple(held))
    return held, orders, stages


def together(*values):
    return lax.optimization_barrier(values)


def tied(value, *others):
    return lax.optimization_barrier((value,) + others)[0]


def decay_table(held, order):
    logs = held[:, N, :384].astype(f32).reshape(-1, 3, 128).sum(axis=1)
    count = logs.shape[0]
    place = [order.index(k) for k in range(count)]
    return jnp.stack([logs[i] for i in place])


def joined_states(held, orders, logs, forward):
    count, mine = logs.shape[0], lax.axis_index("seq")
    who = jnp.arange(count) ^ mine
    if forward:
        counts = who < mine
        between = (who[None] > who[:, None]) & (who[None] < mine)
    else:
        counts = who > mine
        between = (who[None] < who[:, None]) & (who[None] > mine)
    power = jnp.sum(jnp.where(between[:, :, None], logs[None], 0.0), axis=1)
    factor = jnp.where(counts[:, None], jnp.exp2(power), 0.0)
    factor = jnp.repeat(factor[:, :H], P_SIZE, axis=1)
    half = E // 2
    sides = []
    for side in range(2):
        total = 0.0
        for i, k in enumerate(orders[side]):
            weight = factor[k, side * half : (side + 1) * half]
            total = total + weight[None] * held[side][i, :N].astype(f32)
        sides.append(total)
    return jnp.concatenate(sides, axis=1)


def cut(value, width, side):
    return lax.dynamic_slice_in_dim(value, side * width, width, 1)


def gathered(piece):
    return lax.all_gather(piece, "fsdp", axis=0, tiled=True)


def both_cores(mine):
    return mine, swapped(mine, "seq", 1)


def far_product(left, right, width, core):
    return tn(left, cut(right, width, 1 - core)).astype(bf16)


def half_product(left, right, width, core, there):
    came = swapped(there, "seq", 1)
    return (tn(left, cut(right, width, core)) + came.astype(f32)).astype(bf16)


def part_sum(value):
    return lax.psum_scatter(value, "fsdp", scatter_dimension=0, tiled=True)


def added(value, bit):
    return (value.astype(f32) + swapped(value, "seq", bit).astype(f32)).astype(bf16)


def plane_step(first, second, k):
    bits = bits_of("seq")[1:]
    return added(first, bits[k]), added(second, bits[-1 - k])


def plane_sum(first, second):
    for k in range(len(bits_of("seq")) - 1):
        first, second = plane_step(first, second, k)
    return first, second


def swapped_pair(value):
    return value, swapped(value, "seq", 1)


def big_of(mine, other, core):
    def both(low, high):
        return ordered(mine[:, low:high], other[:, low:high], core)

    at = HZ + 2 * HD
    gate, conv = both(0, HZ), both(at, at + HX)
    tops, bottoms = both(HZ, HZ + HD), both(HZ + HD, at)
    steps = mine[:, at + HX : at + HX + H]
    return (
        jnp.concatenate([gate, conv, steps], axis=1).astype(f32),
        jnp.concatenate([tops, bottoms]).astype(f32),
    )


def plane_sum_rows(value):
    half = value.shape[0] // 2
    return jnp.concatenate(plane_sum(value[:half], value[half:]))


def ordered(mine, other, core):
    return jnp.concatenate(
        [jnp.where(core == 0, mine, other), jnp.where(core == 0, other, mine)], axis=1
    )


def reduced_small(value):
    parts, mine = lax.axis_size("fsdp"), lax.axis_index("fsdp")
    bit = parts // 2
    while bit:
        value = value.reshape((2, value.shape[0] // 2) + value.shape[1:])
        upper = (mine & bit) != 0
        kept = jnp.where(upper, value[1], value[0])
        value = kept + swapped(jnp.where(upper, value[0], value[1]), "fsdp", bit)
        bit //= 2
    for bit in bits_of("seq"):
        value = value + swapped(value, "seq", bit)
    return value[0]


def pad_lanes(value):
    return jnp.pad(value, ((0, 0), (0, 128 - value.shape[1])))


def token_table(doc, edge_ids):
    t = doc.shape[0]
    widened = jnp.concatenate([edge_ids, doc, jnp.full((K - 1,), -1, doc.dtype)])
    ids = [widened[k : k + t] == doc for k in range(K - 1)]
    ids += [widened[K - 1 + (K - 1 - k) :][:t] == doc for k in range(K - 1)]
    before = widened[K - 2 : K - 2 + t].reshape(t // Q, Q)[:, :1]
    blocks = doc.reshape(t // Q, Q)
    ids.append((blocks == before).reshape(t))
    ids.append((blocks == blocks[:, Q - 1 :]).reshape(t))
    cols_in = [v.astype(f32) for v in ids] + [doc.astype(f32)]
    table = pad_lanes(jnp.stack(cols_in, axis=1))
    return table, jnp.broadcast_to(doc.astype(f32)[None], (8, t))


def constants():
    spread = np.zeros((128, E), np.float32)
    for h in range(H):
        spread[h, h * P_SIZE : (h + 1) * P_SIZE] = 1
    hot = np.zeros((PAIRS, 2 * Q, 128), np.float32)
    sel = np.zeros((PAIRS, HP, 2 * Q), np.float32)
    for p in range(PAIRS):
        for i in range(2):
            hot[p, i * Q : (i + 1) * Q, 2 * p + i] = 1
            sel[p, 2 * p + i, i * Q : (i + 1) * Q] = 1
    return tuple(
        jnp.asarray(v, bf16) for v in (np.concatenate([spread, spread]), spread.T, hot, sel)
    )


SMALL = (K * CV, CV, H, H, H, D, E)


def local(
    first_tier_source,
    token_articles,
    extra_spikes,
    upstream_gradient,
    entering_projection,
    exit_projection,
    filter_kernels,
    filter_shifts,
    stride_shifts,
    log_shrink_rates,
    bypass_coefficient,
    entry_scaling_gains,
    gated_scaling_gains,
):
    current = first_tier_source[0]
    doc = token_articles[0]
    spike = pad_lanes(extra_spikes[0])
    t = doc.shape[0]
    layers = entering_projection.shape[0]
    parts = lax.axis_size("fsdp")
    e2, et, hot, sel = constants()
    edge_ids = passed_along(doc[t - (K - 1) :], "seq", 1)
    tok, doct = token_table(doc, edge_ids)

    small = (
        filter_kernels, filter_shifts, stride_shifts, log_shrink_rates, bypass_coefficient,
        entry_scaling_gains, gated_scaling_gains,
    )
    flat = jnp.concatenate([v.reshape(layers, -1) for v in small], axis=1)
    flat = lax.all_gather(flat, "fsdp").astype(f32)

    def small_of(layer):
        found, at = [], 0
        for size in SMALL:
            width = size // parts
            found.append(flat[:, layer, at : at + width])
            at += width
        taps = found[0].reshape(parts, K, CV // parts).transpose(1, 0, 2).reshape(K, CV)
        return [taps] + [v.reshape(-1) for v in found[1:]]

    core = lax.axis_index("seq") & 1
    cores = jnp.reshape(core, (1,)).astype(jnp.int32)
    bits = bits_of("seq")
    found = []
    for i in range(layers):
        w = entering_projection[i]
        steps = jnp.pad(w[:, E + CV :], ((0, 0), (0, 128 - H)))
        piece = jnp.concatenate([cut(w[:, E : E + CV], HX, core), steps], axis=1)
        gate, out = cut(w[:, :E], HZ, core), cut(exit_projection[i], HD, core)
        if i == 0:
            found.append((gathered(piece), gathered(gate), gathered(out)))
        else:
            rest = out.shape[0] // 2
            both = gathered(jnp.concatenate([gate, out[:rest], out[rest:]], axis=1))
            found.append((gathered(piece), both, None))
    weights = []
    kept = []
    for i in range(layers):
        wx = found[i][0]
        wx = both_cores(wx if i == 0 else tied(wx, current))
        taps, shifts, strides, rates, bypass, gain_in, gain_out = small_of(i)
        cw = jnp.concatenate([taps, shifts[None], jnp.zeros((3, CV), f32)])
        pv = jnp.concatenate(
            [pad_lanes(jnp.stack([strides, jnp.exp(rates)])), jnp.zeros((6, 128), f32)]
        )
        skip = jnp.repeat(bypass, P_SIZE)[None]
        gain_in, gain_out = gain_in[None], gain_out[None]
        normed, xc, dtr = project(cores, current, gain_in, *wx)
        edge = passed_along(xc[t - (K - 1) :], "seq", 1).astype(f32)
        edge = jnp.concatenate([jnp.zeros((8 - (K - 1), CV), f32), edge])
        pre, x, bc, dt, cum, cumt, dtt, packed = prepare(xc, edge, cw, dtr, spike, tok, pv, e2)
        yi = within(x, bc, cum, cumt, dtt, tok, doct)
        held, orders, stages = all_states(packed, lambda before: yi)
        if i == 0:
            wz, wo = tied(found[i][1], x), tied(found[i][2], *stages[1])
        else:
            both = tied(found[i][1], *stages[1])
            wz, wo = both[:, :HZ], both[:, HZ:].reshape(parts, -1, 2, HD)
            wo = wo.transpose(0, 2, 1, 3).reshape(E, HD)
        wz, wo = both_cores(wz), both_cores(wo)
        weights.append((wx, wz, wo))
        z = project_gate(cores, tied(normed, *stages[0]), *wz)
        logs = decay_table(held[0], orders[0])
        incoming = joined_states(held, orders, logs, True)
        out_type = bf16 if i == layers - 1 else f32
        y, low, new, prior = across(
            cores, yi, x, bc, dt, cum, tok, z, incoming, skip, gain_out, *wo, current, e2, out_type
        )
        kept.append(
            (current, normed, z, xc, dtr, edge, pre, x, bc, dt, cum, cumt, logs, y, low, prior,
             cw, pv, skip, gain_in, gain_out)
        )
        current = new
    grad = upstream_gradient[0]
    results = [None] * layers
    waiting = {}
    for i in reversed(range(layers)):
        wx, wz, wo = weights[i]
        (source, normed, z, xc, dtr, edge, pre, x, bc, dt, cum, cumt, logs, y, low, prior,
         cw, pv, skip, gain_in, gain_out) = kept[i]
        dy, dz, gb, acc, state = open_back(
            cores, grad, *wo, y, z, x, bc, cum, tok, gain_out, e2
        )
        far_gate = far_product(normed, dz, HZ, core)
        far_out = far_product(low, gb, HD, core)
        shared = (bc, dt, cum, cumt, tok, doct, hot, sel)
        near0 = within_back(tied(x, far_gate, far_out), dy, *shared, 0)
        top = waiting.get(i + 1)
        near1 = []

        def second_half(before):
            near1.extend(within_back(tied(x, near0[2], *before), dy, *shared, 1))
            return near1[2]

        held, orders, stages = all_states(state, lambda before: near0[2], second_half)
        half_gate = half_product(normed, tied(dz, near1[2]), HZ, core, far_gate)
        half_out = half_product(low, tied(gb, near1[2]), HD, core, far_out)
        grad_out, grad_gate = part_sum(half_out), part_sum(half_gate)
        later = joined_states(held, orders, logs, False)
        later = tied(later, half_out, half_gate)
        if top is not None:
            sums = plane_step(*tied(top, *stages[0]), 0)
        dxc, cacc, hacc, first = across_back(
            x, pre, xc, edge, bc, dy, near0, near1, dt, cum, dtr, tok, prior, later, skip, cw, pv, e2, et
        )
        if top is not None:
            first, sums = together(first, sums)
        first, grad_out = together(first, grad_out)
        masked = [first[: K - 1] * tok[: K - 1, k : k + 1] for k in range(K - 1)]
        borrowed = jnp.stack(
            [sum(cw[k] * masked[k][e - k] for k in range(e + 1)) for e in range(K - 1)]
        )
        back = passed_along(borrowed, "seq", -1)
        gap = jnp.zeros((K - 1, 128), f32)
        back = jnp.concatenate([back[:, :HX], gap, back[:, HX:], gap], axis=1)
        mended = (dxc[t - (K - 1) :].astype(f32) + back).astype(bf16)
        dxc = dxc.at[t - (K - 1) :].set(mended)
        dxc, grad_gate = together(dxc, grad_gate)
        far_conv = far_product(normed, dxc, CX, core)
        conv_half = half_product(normed, dxc, CX, core, far_conv)
        rest = grad_out.shape[0] // 2
        grad_out = jnp.concatenate([grad_out[:rest], grad_out[rest:]], axis=1)
        if i == 0:
            early = plane_sum(*tied((grad_gate, grad_out), far_conv))
            grad = tied(grad, conv_half, *early)
            early = swapped_pair(jnp.concatenate(early, axis=1))
            if top is not None:
                for k in range(1, len(bits) - 1):
                    sums = plane_step(*sums, k)
                results[i + 1] = results[i + 1] + (swapped_pair(jnp.concatenate(sums)),)
        grad, nacc = close_back(cores, dz, dxc, wz, wx, source, gain_in, grad)
        grad_conv = part_sum(conv_half)
        if i > 0:
            grad = tied(grad, conv_half)
            value = jnp.concatenate([grad_gate, grad_out, grad_conv], axis=1)
            half = value.shape[0] // 2
            waiting[i] = (value[:half], value[half:])
        tiny = [
            cacc[:K], cacc[K], hacc[0, :H], hacc[1, :H],
            jnp.sum(acc[1].reshape(H, P_SIZE), axis=1), nacc[0], acc[0],
        ]
        results[i] = (tiny,)
    packed = []
    for i in range(layers):
        tiny = results[i][0]
        taps = tiny[0].reshape(K, parts, CV // parts).transpose(1, 0, 2).reshape(parts, -1)
        packed.append(jnp.concatenate([taps] + [v.reshape(parts, -1) for v in tiny[1:]], axis=1))
    mine = reduced_small(jnp.stack(packed, axis=1))
    late = swapped_pair(plane_sum_rows(grad_conv))
    results[0] += (tuple(jnp.concatenate(v, axis=1) for v in zip(early, late)),)
    bigs = [big_of(*results[i][1], core) for i in range(layers)]
    smalls, at = [], 0
    for size in SMALL:
        width = size // parts
        smalls.append(mine[:, at : at + width])
        at += width
    smalls[0] = smalls[0].reshape(layers, K, CV // parts)
    bigs = [jnp.stack([v[j] for v in bigs]) for j in range(2)]
    return (current[None], grad[None], *bigs, *smalls)


def solution(mesh):
    placed = (
        P("fsdp", "seq", None),
        P("fsdp", "seq"),
        P("fsdp", "seq", None),
        P("fsdp", "seq", None),
        P(None, "fsdp", None),
        P(None, "fsdp", None),
        P(None, None, "fsdp"),
        P(None, "fsdp"),
        P(None, "fsdp"),
        P(None, "fsdp"),
        P(None, "fsdp"),
        P(None, "fsdp"),
        P(None, "fsdp"),
    )
    return jax.shard_map(
        local,
        mesh=mesh,
        in_specs=placed,
        out_specs=(
            P("fsdp", "seq", None),
            P("fsdp", "seq", None),
            P(None, "fsdp", None),
            P(None, "fsdp", None),
            P(None, None, "fsdp"),
            P(None, "fsdp"),
            P(None, "fsdp"),
            P(None, "fsdp"),
            P(None, "fsdp"),
            P(None, "fsdp"),
            P(None, "fsdp"),
        ),
        check_vma=False,
    )
```

```python
from functools import partial

import jax
import jax.numpy as jnp
import numpy as np
from jax import lax
from jax.experimental import pallas as pl
from jax.experimental.pallas import tpu as pltpu
from jax.sharding import PartitionSpec as P

D = 768
H = 24
P_SIZE = 64
N = 128
K = 4
E = 1536
CV = 1792
HX = CV // 2
HZ = E // 2
HD = D // 2
CX = HX + 128
Q = 128
TT = 256
SUB = TT // Q
W = 256
HP = 32
PAIRS = H // 2
eps = 1e-05
LOG2E = 1.4426950408889634
BIG = -1e30
CUT = 30000.0
f32 = jnp.float32
bf16 = jnp.bfloat16
highest = lax.Precision.HIGHEST
VMEM_LIMIT = 56 * 1024 * 1024


def nn(a, b):
    return lax.dot_general(a, b, (((1,), (0,)), ((), ())), preferred_element_type=f32)


def nt(a, b):
    return lax.dot_general(a, b, (((1,), (1,)), ((), ())), preferred_element_type=f32)


def tn(a, b):
    return lax.dot_general(a, b, (((0,), (0,)), ((), ())), preferred_element_type=f32)


def nn_exact(a, b):
    return lax.dot_general(
        a, b, (((1,), (0,)), ((), ())), precision=highest, preferred_element_type=f32
    )


def halves(v):
    hi = v.astype(bf16)
    lo = (v - hi.astype(f32)).astype(bf16)
    return jnp.concatenate([hi, lo], axis=1)


def sigmoid(v):
    return 0.5 + 0.5 * jnp.tanh(0.5 * v)


def softplus(v):
    return jnp.maximum(v, 0.0) + jnp.log1p(jnp.exp(-jnp.abs(v)))


def iota2(shape, dim):
    return lax.broadcasted_iota(jnp.int32, shape, dim)


def lane_halves():
    lane = iota2((1, 2 * P_SIZE), 1)
    left = (lane < P_SIZE).astype(f32).astype(bf16)
    right = (lane >= P_SIZE).astype(f32).astype(bf16)
    return left, right


def full(shape):
    return pl.BlockSpec(shape, lambda i: (0,) * len(shape))


def rows(width, size=TT):
    return pl.BlockSpec((size, width), lambda i: (i, 0))


def cols(height):
    return pl.BlockSpec((height, TT), lambda i: (0, i))


def params():
    return pltpu.CompilerParams(vmem_limit_bytes=VMEM_LIMIT, dimension_semantics=("arbitrary",))


def cost(micros):
    return pl.CostEstimate(
        flops=int(micros * 1e9), bytes_accessed=int(micros * 3e6), transcendentals=0
    )


SMEM = pl.BlockSpec(memory_space=pltpu.SMEM)


def sides(core_ref, width):
    mine = core_ref[0] * width
    return pl.ds(pl.multiple_of(mine, 128), width), pl.ds(
        pl.multiple_of(width - mine, 128), width
    )


def shape(dims, dtype):
    return jax.ShapeDtypeStruct(dims, dtype)


def project_kernel(core_ref, x_ref, gain_ref, mine_ref, other_ref, normed_ref, xc_ref, dtr_ref):
    x = x_ref[...].astype(f32)
    scale = lax.rsqrt(jnp.mean(x * x, axis=-1, keepdims=True) + eps)
    normed = (x * scale * gain_ref[...]).astype(bf16)
    normed_ref[...] = normed
    own, far = sides(core_ref, HX)
    xc_ref[:, own] = nn(normed, mine_ref[:, :HX]).astype(bf16)
    dtr_ref[...] = nn(normed, mine_ref[:, HX:])
    xc_ref[:, far] = nn(normed, other_ref[:, :HX]).astype(bf16)


def project(core, x, gain, mine, other):
    t = x.shape[0]
    return pl.pallas_call(
        project_kernel,
        grid=(t // TT,),
        in_specs=[SMEM, rows(D), full((1, D)), full((D, CX)), full((D, CX))],
        out_specs=[rows(D), rows(CV), rows(128)],
        out_shape=[shape((t, D), bf16), shape((t, CV), bf16), shape((t, 128), f32)],
        compiler_params=params(),
        cost_estimate=cost(8),
        name="project",
    )(core, x, gain, mine, other)


def gate_kernel(core_ref, normed_ref, mine_ref, other_ref, z_ref):
    own, far = sides(core_ref, HZ)
    z_ref[:, own] = nn(normed_ref[...], mine_ref[...]).astype(bf16)
    z_ref[:, far] = nn(normed_ref[...], other_ref[...]).astype(bf16)


def project_gate(core, normed, mine, other):
    t = normed.shape[0]
    return pl.pallas_call(
        gate_kernel,
        grid=(t // TT,),
        in_specs=[SMEM, rows(D), full((D, HZ)), full((D, HZ))],
        out_specs=rows(E),
        out_shape=shape((t, E), bf16),
        compiler_params=params(),
        cost_estimate=cost(6),
        name="project_gate",
    )(core, normed, mine, other)


def prepare_kernel(
    xc_ref, edge_ref, cw_ref, dtr_ref, spike_ref, tok_ref, pv_ref, e2_ref,
    pre_ref, x_ref, bc_ref, dt_ref, cum_ref, cumt_ref, dtt_ref, packed_ref,
    ext, state_ref, carry_ref,
):
    step = pl.program_id(0)

    @pl.when(step == 0)
    def _():
        ext[0:8, :] = edge_ref[...]
        state_ref[...] = jnp.zeros_like(state_ref)
        carry_ref[...] = jnp.zeros_like(carry_ref)

    @pl.when(step > 0)
    def _():
        ext[0:8, :] = ext[TT : TT + 8, :]

    ext[8 : TT + 8, :] = xc_ref[...].astype(f32)
    masks = [tok_ref[:, k : k + 1] for k in range(K - 1)]
    for b in range(CV // 128):
        at = slice(b * 128, (b + 1) * 128)
        total = cw_ref[K : K + 1, at] + cw_ref[K - 1 : K, at] * ext[8 : TT + 8, at]
        for k in range(K - 1):
            total = total + cw_ref[k : k + 1, at] * (ext[5 + k : 5 + k + TT, at] * masks[k])
        pre_ref[:, at] = total.astype(bf16)
        act = (total * sigmoid(total)).astype(bf16)
        if b < E // 128:
            x_ref[:, at] = act
        else:
            bc_ref[:, (b - E // 128) * 128 : (b - E // 128 + 1) * 128] = act

    dt = softplus(dtr_ref[...] + pv_ref[0:1, :])
    log_decay = (spike_ref[...] - dt * pv_ref[1:2, :]) * LOG2E
    dt_ref[...] = dt
    dtt_ref[...] = jnp.transpose(dt)[:HP, :]
    lower = (iota2((Q, Q), 0) >= iota2((Q, Q), 1)).astype(f32)
    for s in range(SUB):
        r = slice(s * Q, (s + 1) * Q)
        cum = nn_exact(lower, log_decay[r])
        cum_ref[r, :] = cum
        cumt_ref[:, r] = jnp.transpose(cum)[:HP, :]
        last = cum[Q - 1 : Q, :]
        tail = jnp.exp2(last - cum) * tok_ref[r, 7:8] * dt[r]
        kept = tok_ref[s * Q + Q - 1 : s * Q + Q, 6:7]
        carried = jnp.exp2(last) * kept
        carry_ref[...] = carry_ref[...] + (last + (kept - 1.0) * CUT)
        wide = jnp.concatenate([tail, jnp.broadcast_to(carried, (16, 128))], axis=0)
        wide = halves(wide)
        b_in = bc_ref[r, :N]
        for b in range(E // W):
            at = slice(b * W, (b + 1) * W)
            grown = nn(wide, e2_ref[:, at])
            weighted = (x_ref[r, at].astype(f32) * grown[:Q]).astype(bf16)
            state_ref[:, at] = state_ref[:, at] * grown[Q : Q + 1] + tn(b_in, weighted)

    @pl.when(step == pl.num_programs(0) - 1)
    def _():
        packed_ref[:N, :] = state_ref[...].astype(bf16)
        packed_ref[N:, :] = jnp.zeros((16, E), bf16)
        rest = jnp.concatenate([carry_ref[...], carry_ref[...]], axis=0)
        for k in range(3):
            part = rest.astype(bf16)
            packed_ref[N:, k * 128 : (k + 1) * 128] = part
            rest = rest - part.astype(f32)


def prepare(xc, edge, cw, dtr, spike, tok, pv, e2):
    t = xc.shape[0]
    return pl.pallas_call(
        prepare_kernel,
        grid=(t // TT,),
        in_specs=[
            rows(CV), full((8, CV)), full((8, CV)), rows(128), rows(128), rows(128),
            full((8, 128)), full((256, E)),
        ],
        out_specs=[
            rows(CV), rows(E), rows(2 * N), rows(128), rows(128), cols(HP), cols(HP),
            full((N + 16, E)),
        ],
        out_shape=[
            shape((t, CV), bf16),
            shape((t, E), bf16),
            shape((t, 2 * N), bf16),
            shape((t, 128), f32),
            shape((t, 128), f32),
            shape((HP, t), f32),
            shape((HP, t), f32),
            shape((N + 16, E), bf16),
        ],
        scratch_shapes=[
            pltpu.VMEM((TT + 8, CV), f32),
            pltpu.VMEM((N, E), f32),
            pltpu.VMEM((8, 128), f32),
        ],
        compiler_params=params(),
        cost_estimate=cost(15),
        name="prepare",
    )(xc, edge, cw, dtr, spike, tok, pv, e2)


def within_kernel(x_ref, bc_ref, cum_ref, cumt_ref, dtt_ref, tok_ref, doct_ref, y_ref):
    left, right = lane_halves()
    order = iota2((Q, Q), 0) >= iota2((Q, Q), 1)
    for s in range(SUB):
        r = slice(s * Q, (s + 1) * Q)
        same = tok_ref[r, 8:9] == doct_ref[0:1, r]
        bias = jnp.where(order & same, 0.0, BIG)
        scores = nt(bc_ref[r, N:], bc_ref[r, :N])
        cum = cum_ref[r, :]
        for p in range(PAIRS):
            at = slice(p * 128, (p + 1) * 128)
            xp = x_ref[r, at]
            mixes = []
            for h in (2 * p, 2 * p + 1):
                gap = (cum[:, h : h + 1] - cumt_ref[h : h + 1, r]) + bias
                mixes.append((jnp.exp2(gap) * (scores * dtt_ref[h : h + 1, r])).astype(bf16))
            both = jnp.concatenate([xp * left, xp * right], axis=0)
            y_ref[r, at] = nn(jnp.concatenate(mixes, axis=1), both).astype(bf16)


def within(x, bc, cum, cumt, dtt, tok, doct):
    t = x.shape[0]
    return pl.pallas_call(
        within_kernel,
        grid=(t // TT,),
        in_specs=[rows(E), rows(2 * N), rows(128), cols(HP), cols(HP), rows(128), cols(8)],
        out_specs=rows(E),
        out_shape=shape((t, E), bf16),
        compiler_params=params(),
        cost_estimate=cost(8),
        name="within",
    )(x, bc, cum, cumt, dtt, tok, doct)


def across_kernel(
    core_ref, yi_ref, x_ref, bc_ref, dt_ref, cum_ref, tok_ref, z_ref, first_ref, skip_ref,
    gain_ref, mine_ref, other_ref, res_ref, e2_ref,
    y_ref, low_ref, new_ref, prior_ref,
    state, gated,
):
    step = pl.program_id(0)

    @pl.when(step == 0)
    def _():
        state[...] = first_ref[...]

    for s in range(SUB):
        r = slice(s * Q, (s + 1) * Q)
        cum = cum_ref[r, :]
        last = cum[Q - 1 : Q, :]
        tail = jnp.exp2(last - cum) * tok_ref[r, 7:8] * dt_ref[r, :]
        head = jnp.exp2(cum) * tok_ref[r, 6:7]
        carried = head[Q - 1 : Q, :]
        wide = halves(
            jnp.concatenate([tail, head, jnp.broadcast_to(carried, (16, 128))], axis=0)
        )
        b_in = bc_ref[r, :N]
        c_out = bc_ref[r, N:]
        square = jnp.zeros((Q, W), f32)
        for b in range(E // W):
            at = slice(b * W, (b + 1) * W)
            grown = nn(wide, e2_ref[:, at])
            xs = x_ref[r, at].astype(f32)
            held = state[:, at]
            prior_ref[s, :, at] = held.astype(bf16)
            y = (
                yi_ref[r, at].astype(f32)
                + nn(c_out, held.astype(bf16)) * grown[Q : 2 * Q]
                + skip_ref[0:1, at] * xs
            )
            y_ref[r, at] = y.astype(bf16)
            z = z_ref[r, at].astype(f32)
            made = y * (z * sigmoid(z))
            gated[r, at] = made
            square = square + made * made
            weighted = (xs * grown[:Q]).astype(bf16)
            state[:, at] = held * grown[2 * Q : 2 * Q + 1] + tn(b_in, weighted)
        scale = lax.rsqrt(jnp.sum(square, axis=-1, keepdims=True) * (1.0 / E) + eps)
        for b in range(E // W):
            at = slice(b * W, (b + 1) * W)
            low_ref[r, at] = (gated[r, at] * scale * gain_ref[0:1, at]).astype(bf16)
    for at, w_ref in zip(sides(core_ref, HD), (mine_ref, other_ref)):
        new = res_ref[:, at].astype(f32) + nn(low_ref[...], w_ref[...])
        new_ref[:, at] = new.astype(new_ref.dtype)


def across(core, yi, x, bc, dt, cum, tok, z, first, skip, gain, mine, other, res, e2, out_type):
    t = x.shape[0]
    return pl.pallas_call(
        across_kernel,
        grid=(t // TT,),
        in_specs=[
            SMEM, rows(E), rows(E), rows(2 * N), rows(128), rows(128), rows(128), rows(E),
            full((N, E)), full((1, E)), full((1, E)), full((E, HD)), full((E, HD)), rows(D),
            full((256, E)),
        ],
        out_specs=[rows(E), rows(E), rows(D), pl.BlockSpec((SUB, N, E), lambda i: (i, 0, 0))],
        out_shape=[
            shape((t, E), bf16),
            shape((t, E), bf16),
            shape((t, D), out_type),
            shape((t // Q, N, E), bf16),
        ],
        scratch_shapes=[pltpu.VMEM((N, E), f32), pltpu.VMEM((TT, E), f32)],
        compiler_params=params(),
        cost_estimate=cost(16),
        name="across",
    )(core, yi, x, bc, dt, cum, tok, z, first, skip, gain, mine, other, res, e2)


def open_back_kernel(
    core_ref, g_ref, mine_ref, other_ref, y_ref, z_ref, x_ref, bc_ref, cum_ref, tok_ref,
    gain_ref, e2_ref,
    dy_ref, dz_ref, gb_ref, acc_ref, low_ref,
    held, state_ref,
):
    step = pl.program_id(0)

    @pl.when(step == 0)
    def _():
        acc_ref[...] = jnp.zeros_like(acc_ref)
        state_ref[...] = jnp.zeros_like(state_ref)

    gb_ref[...] = g_ref[...].astype(bf16)
    own, far = sides(core_ref, HD)
    held[...] = nt(gb_ref[:, own], mine_ref[...]) + nt(gb_ref[:, far], other_ref[...])
    for s in reversed(range(SUB)):
        r = slice(s * Q, (s + 1) * Q)
        square = jnp.zeros((Q, W), f32)
        cross = jnp.zeros((Q, W), f32)
        for b in range(E // W):
            at = slice(b * W, (b + 1) * W)
            z = z_ref[r, at].astype(f32)
            gated = y_ref[r, at].astype(f32) * (z * sigmoid(z))
            square = square + gated * gated
            cross = cross + gated * (held[r, at] * gain_ref[0:1, at])
        scale = lax.rsqrt(jnp.sum(square, axis=-1, keepdims=True) * (1.0 / E) + eps)
        pull = (scale * scale * scale) * (jnp.sum(cross, axis=-1, keepdims=True) * (1.0 / E))
        cum = cum_ref[r, :]
        head = jnp.exp2(cum) * tok_ref[r, 6:7]
        wide = halves(
            jnp.concatenate([head, jnp.broadcast_to(head[Q - 1 : Q, :], (16, 128))], axis=0)
        )
        c_out = bc_ref[r, N:]
        for b in range(E // W):
            at = slice(b * W, (b + 1) * W)
            z = z_ref[r, at].astype(f32)
            gate = sigmoid(z)
            y = y_ref[r, at].astype(f32)
            gated = y * (z * gate)
            dn = held[r, at]
            acc_ref[0:1, at] += jnp.sum(dn * (gated * scale), axis=0, keepdims=True)
            dgated = scale * (dn * gain_ref[0:1, at]) - gated * pull
            dy = dgated * (z * gate)
            dz_ref[r, at] = (dgated * y * (gate * (1.0 + z * (1.0 - gate)))).astype(bf16)
            acc_ref[1:2, at] += jnp.sum(dy * x_ref[r, at].astype(f32), axis=0, keepdims=True)
            dy_ref[r, at] = dy.astype(bf16)
            grown = nn(wide, e2_ref[:, at])
            state_ref[:, at] = state_ref[:, at] * grown[Q : Q + 1] + tn(
                c_out, (dy * grown[:Q]).astype(bf16)
            )

    @pl.when(step == pl.num_programs(0) - 1)
    def _():
        low_ref[...] = state_ref[...].astype(bf16)


def open_back(core, g, mine, other, y, z, x, bc, cum, tok, gain, e2):
    t = x.shape[0]
    n = t // TT

    def turned(width):
        return pl.BlockSpec((TT, width), lambda i: (n - 1 - i, 0))

    return pl.pallas_call(
        open_back_kernel,
        grid=(n,),
        in_specs=[
            SMEM, turned(D), full((E, HD)), full((E, HD)), turned(E), turned(E), turned(E),
            turned(2 * N), turned(128), turned(128), full((1, E)), full((256, E)),
        ],
        out_specs=[turned(E), turned(E), turned(D), full((8, E)), full((N, E))],
        out_shape=[
            shape((t, E), bf16),
            shape((t, E), bf16),
            shape((t, D), bf16),
            shape((8, E), f32),
            shape((N, E), bf16),
        ],
        scratch_shapes=[pltpu.VMEM((TT, E), f32), pltpu.VMEM((N, E), f32)],
        compiler_params=params(),
        cost_estimate=cost(20),
        name="open_back",
    )(core, g, mine, other, y, z, x, bc, cum, tok, gain, e2)


def within_back_kernel(
    pairs,
    x_ref, dy_ref, bc_ref, dt_ref, cum_ref, cumt_ref, tok_ref, doct_ref, hot_ref, sel_ref,
    dxdt_ref, dbc_ref, cross_ref,
):
    left, right = lane_halves()
    order = iota2((Q, Q), 1) >= iota2((Q, Q), 0)
    suffix = order.astype(f32)
    for s in range(SUB):
        r = slice(s * Q, (s + 1) * Q)
        same = tok_ref[r, 8:9] == doct_ref[0:1, r]
        bias = jnp.where(order & same, 0.0, BIG)
        b_in = bc_ref[r, :N]
        c_out = bc_ref[r, N:]
        scores = nt(b_in, c_out)
        cum = cum_ref[r, :]
        dt = dt_ref[r, :]
        grad_scores = jnp.zeros((Q, Q), f32)
        by_source = jnp.zeros((Q, 128), f32)
        by_target = jnp.zeros((HP, Q), f32)
        for p in pairs:
            at = slice((p - pairs[0]) * 128, (p - pairs[0] + 1) * 128)
            xp = x_ref[r, at]
            dyp = dy_ref[r, at]
            dmix = nt(jnp.concatenate([xp * left, xp * right], axis=0), dyp)
            mixes = []
            flows = []
            for i in range(2):
                h = 2 * p + i
                decay = jnp.exp2((cumt_ref[h : h + 1, r] - cum[:, h : h + 1]) + bias)
                mixes.append((decay * scores).astype(bf16))
                part = dmix[i * Q : (i + 1) * Q] * (decay * dt[:, h : h + 1])
                grad_scores = grad_scores + part
                flows.append((part * scores).astype(bf16))
            both = jnp.concatenate([dyp * left, dyp * right], axis=0)
            dxdt_ref[r, at] = nn(jnp.concatenate(mixes, axis=1), both).astype(bf16)
            by_source = by_source + nn(
                jnp.concatenate(flows, axis=1), hot_ref[p - pairs[0]]
            )
            by_target = by_target + nn(
                sel_ref[p - pairs[0]], jnp.concatenate(flows, axis=0)
            )
        low = grad_scores.astype(bf16)
        dbc_ref[r, :N] = nn(low, c_out)
        dbc_ref[r, N:] = tn(low, b_in)
        target = jnp.transpose(
            jnp.concatenate([by_target, jnp.zeros((128 - HP, Q), f32)], axis=0)
        )
        cross_ref[r, :] = nn_exact(suffix, target - by_source)


def within_back(x, dy, bc, dt, cum, cumt, tok, doct, hot, sel, part):
    t = x.shape[0]
    size = PAIRS // 2
    half = pl.BlockSpec((TT, HZ), lambda i: (i, part))
    return pl.pallas_call(
        partial(within_back_kernel, range(part * size, (part + 1) * size)),
        grid=(t // TT,),
        in_specs=[
            half, half, rows(2 * N), rows(128), rows(128), cols(HP), rows(128), cols(8),
            pl.BlockSpec((size,) + hot.shape[1:], lambda i: (part, 0, 0)),
            pl.BlockSpec((size,) + sel.shape[1:], lambda i: (part, 0, 0)),
        ],
        out_specs=[rows(HZ), rows(2 * N), rows(128)],
        out_shape=[shape((t, HZ), bf16), shape((t, 2 * N), f32), shape((t, 128), f32)],
        compiler_params=params(),
        cost_estimate=cost(12),
        name="within_back",
    )(x, dy, bc, dt, cum, cumt, tok, doct, hot, sel)


def across_back_kernel(
    x_ref, pre_ref, xc_ref, halo_ref, edge_ref, bc_ref, dy_ref, dxdt0_ref, dxdt1_ref,
    dbc0_ref, dbc1_ref, cross0_ref, cross1_ref,
    dt_ref, cum_ref, dtr_ref, tok_ref, prior_ref, last_ref, skip_ref, cw_ref, pv_ref, e2_ref,
    et_ref,
    dxc_ref, cacc_ref, hacc_ref, first_ref,
    state, dp, ext,
):
    step = pl.program_id(0)
    count = pl.num_programs(0)

    @pl.when(step == 0)
    def _():
        state[...] = last_ref[...]
        cacc_ref[...] = jnp.zeros_like(cacc_ref)
        hacc_ref[...] = jnp.zeros_like(hacc_ref)
        dp[TT : TT + 8, :] = jnp.zeros((8, CV), f32)

    @pl.when(step > 0)
    def _():
        dp[TT : TT + 8, :] = dp[0:8, :]

    @pl.when(step == count - 1)
    def _():
        ext[0:8, :] = edge_ref[...]

    @pl.when(step < count - 1)
    def _():
        ext[0:8, :] = halo_ref[...].astype(f32)[8:16, :]

    def through_silu(grad, r, at):
        v = pre_ref[r, at].astype(f32)
        gate = sigmoid(v)
        dp[r, at] = grad * (gate * (1.0 + v * (1.0 - gate)))

    strict = (iota2((Q, Q), 0) > iota2((Q, Q), 1)).astype(f32)
    suffix = (iota2((Q, Q), 0) <= iota2((Q, Q), 1)).astype(f32)
    rate = pv_ref[1:2, :]
    for s in reversed(range(SUB)):
        r = slice(s * Q, (s + 1) * Q)
        cum = cum_ref[r, :]
        dt = dt_ref[r, :]
        last = cum[Q - 1 : Q, :]
        tail = jnp.exp2(last - cum) * tok_ref[r, 7:8]
        head = jnp.exp2(cum) * tok_ref[r, 6:7]
        carried = head[Q - 1 : Q, :]
        wide = halves(
            jnp.concatenate([tail, head, dt, jnp.broadcast_to(carried, (16, 128))], axis=0)
        )
        b_in = bc_ref[r, :N]
        c_out = bc_ref[r, N:]
        grad_b = dbc0_ref[r, :N] + dbc1_ref[r, :N]
        grad_c = dbc0_ref[r, N:] + dbc1_ref[r, N:]
        sums = jnp.zeros((3 * Q + 16, 128), f32)
        for b in range(E // W):
            at = slice(b * W, (b + 1) * W)
            grown = nn(wide, e2_ref[:, at])
            dt_wide = grown[2 * Q : 3 * Q]
            after = state[:, at]
            after_low = after.astype(bf16)
            before = prior_ref[s, :, at]
            xs = x_ref[r, at].astype(f32)
            dy = dy_ref[r, at].astype(f32)
            reach = nn(b_in, after_low) * grown[:Q]
            read = nn(c_out, before)
            near = (dxdt0_ref, dxdt1_ref)[b * W // HZ]
            dxdt = near[r, b * W % HZ : b * W % HZ + W].astype(f32) + reach
            dyg = dy * grown[Q : 2 * Q]
            dyg_low = dyg.astype(bf16)
            joint = jnp.sum(after * before.astype(f32), axis=0, keepdims=True)
            stacked = jnp.concatenate(
                [
                    (xs * dxdt).astype(bf16),
                    (xs * reach).astype(bf16),
                    (dyg * read).astype(bf16),
                    jnp.broadcast_to(joint, (16, W)).astype(bf16),
                ],
                axis=0,
            )
            sums = sums + nn(stacked, et_ref[at, :])
            through_silu(dxdt * dt_wide + skip_ref[0:1, at] * dy, r, at)
            grad_c = grad_c + nt(dyg_low, before)
            grad_b = grad_b + nt((xs * (grown[:Q] * dt_wide)).astype(bf16), after_low)
            state[:, at] = after * grown[3 * Q : 3 * Q + 1] + tn(c_out, dyg_low)
        through_silu(grad_b, r, slice(E, E + N))
        through_silu(grad_c, r, slice(E + N, CV))
        dlog = (
            cross0_ref[r, :]
            + cross1_ref[r, :]
            + nn_exact(strict, sums[Q : 2 * Q] * dt)
            + nn_exact(suffix, sums[2 * Q : 3 * Q])
            + carried * sums[3 * Q : 3 * Q + 1]
        )
        draw = (sums[:Q] - rate * dlog) * sigmoid(dtr_ref[r, :] + pv_ref[0:1, :])
        dxc_ref[r, HX:CX] = draw.astype(bf16)
        dxc_ref[r, CX + HX :] = draw.astype(bf16)
        hacc_ref[0:1, :] += jnp.sum(draw, axis=0, keepdims=True)
        hacc_ref[1:2, :] -= rate * jnp.sum(dt * dlog, axis=0, keepdims=True)

    ext[8 : TT + 8, :] = xc_ref[...].astype(f32)
    masks = [tok_ref[:, k : k + 1] for k in range(K - 1)]
    ahead = [tok_ref[:, 3 + k : 4 + k] for k in range(K - 1)]
    for b in range(CV // 128):
        at = slice(b * 128, (b + 1) * 128)
        own = dp[0:TT, at]
        total = cw_ref[K - 1 : K, at] * own
        cacc_ref[K : K + 1, at] += jnp.sum(own, axis=0, keepdims=True)
        cacc_ref[K - 1 : K, at] += jnp.sum(own * ext[8 : TT + 8, at], axis=0, keepdims=True)
        for k in range(K - 1):
            total = total + cw_ref[k : k + 1, at] * (dp[3 - k : 3 - k + TT, at] * ahead[k])
            cacc_ref[k : k + 1, at] += jnp.sum(
                own * (ext[5 + k : 5 + k + TT, at] * masks[k]), axis=0, keepdims=True
            )
        to = b * 128 + (128 if b * 128 >= HX else 0)
        dxc_ref[:, to : to + 128] = total.astype(bf16)

    @pl.when(step == count - 1)
    def _():
        first_ref[...] = dp[0:8, :]


def across_back(
    x, pre, xc, edge, bc, dy, near0, near1, dt, cum, dtr, tok, prior, last, skip, cw, pv, e2, et
):
    t = x.shape[0]
    n = t // TT

    def turned(width):
        return pl.BlockSpec((TT, width), lambda i: (n - 1 - i, 0))

    halo = pl.BlockSpec((16, CV), lambda i: (jnp.maximum((n - 1 - i) * (TT // 16) - 1, 0), 0))
    return pl.pallas_call(
        across_back_kernel,
        grid=(n,),
        in_specs=[
            turned(E), turned(CV), turned(CV), halo, full((8, CV)), turned(2 * N), turned(E),
            turned(HZ), turned(HZ), turned(2 * N), turned(2 * N), turned(128), turned(128),
            turned(128), turned(128), turned(128), turned(128), pl.BlockSpec((SUB, N, E), lambda i: (n - 1 - i, 0, 0)), full((N, E)),
            full((1, E)), full((8, CV)), full((8, 128)), full((256, E)), full((E, 128)),
        ],
        out_specs=[turned(2 * CX), full((8, CV)), full((8, 128)), full((8, CV))],
        out_shape=[
            shape((t, 2 * CX), bf16),
            shape((8, CV), f32),
            shape((8, 128), f32),
            shape((8, CV), f32),
        ],
        scratch_shapes=[
            pltpu.VMEM((N, E), f32),
            pltpu.VMEM((TT + 8, CV), f32),
            pltpu.VMEM((TT + 8, CV), f32),
        ],
        compiler_params=params(),
        cost_estimate=cost(31),
        name="across_back",
    )(
        x, pre, xc, xc, edge, bc, dy, near0[0], near1[0], near0[1], near1[1], near0[2], near1[2],
        dt, cum, dtr, tok, prior, last, skip, cw, pv, e2, et,
    )


def close_back_kernel(
    core_ref, dz_ref, dxc_ref, zm_ref, zo_ref, xm_ref, xo_ref, x_ref, gain_ref, g_ref,
    new_ref, acc_ref,
):
    @pl.when(pl.program_id(0) == 0)
    def _():
        acc_ref[...] = jnp.zeros_like(acc_ref)

    own_z, far_z = sides(core_ref, HZ)
    own_x, far_x = sides(core_ref, CX)
    dn = (
        nt(dz_ref[:, own_z], zm_ref[...])
        + nt(dz_ref[:, far_z], zo_ref[...])
        + nt(dxc_ref[:, own_x], xm_ref[...])
        + nt(dxc_ref[:, far_x][:, :HX], xo_ref[:, :HX])
    )
    x = x_ref[...].astype(f32)
    scale = lax.rsqrt(jnp.mean(x * x, axis=-1, keepdims=True) + eps)
    acc_ref[0:1, :] += jnp.sum(dn * (x * scale), axis=0, keepdims=True)
    pulled = dn * gain_ref[...]
    mean = jnp.mean(pulled * x, axis=-1, keepdims=True)
    new_ref[...] = g_ref[...].astype(f32) + scale * pulled - x * (scale * scale * scale * mean)


def close_back(core, dz, dxc, zs, xs, x, gain, g):
    t = x.shape[0]
    return pl.pallas_call(
        close_back_kernel,
        grid=(t // TT,),
        in_specs=[
            SMEM, rows(E), rows(2 * CX), full((D, HZ)), full((D, HZ)), full((D, CX)),
            full((D, CX)), rows(D), full((1, D)), rows(D),
        ],
        out_specs=[rows(D), full((8, D))],
        out_shape=[shape((t, D), f32), shape((8, D), f32)],
        compiler_params=params(),
        cost_estimate=cost(12),
        name="close_back",
    )(core, dz, dxc, *zs, *xs, x, gain, g)


def passed_along(value, axis, steps):
    count = lax.axis_size(axis)
    first, last = (max(0, -steps), min(count, count - steps))
    return lax.ppermute(value, axis, [(source, source + steps) for source in range(first, last)])


def swapped(value, axis, bit):
    count = lax.axis_size(axis)
    return lax.ppermute(value, axis, [(source, source ^ bit) for source in range(count)])


def bits_of(axis):
    return [1 << k for k in range((lax.axis_size(axis) - 1).bit_length())]


def all_states(packed, *beside):
    bits = bits_of("seq")
    half = E // 2
    sides = [(packed[:, :half], bits[1:] + bits[:1]), (packed[:, half:], bits[:0:-1] + bits[:1])]
    held = [value[None] for value, _ in sides]
    orders = [[0], [0]]
    stages = []
    for k in range(len(bits)):
        before = tuple(held)
        for side, (_, path) in enumerate(sides):
            came = swapped(held[side], "seq", path[k])
            held[side] = jnp.concatenate([held[side], came])
            orders[side] = orders[side] + [o ^ path[k] for o in orders[side]]
        fill = [make(before) for make in beside[k : k + 1]]
        held = list(together(*held, *fill)[:2])
        stages.append(tuple(held))
    return held, orders, stages


def together(*values):
    return lax.optimization_barrier(values)


def tied(value, *others):
    return lax.optimization_barrier((value,) + others)[0]


def decay_table(held, order):
    logs = held[:, N, :384].astype(f32).reshape(-1, 3, 128).sum(axis=1)
    count = logs.shape[0]
    place = [order.index(k) for k in range(count)]
    return jnp.stack([logs[i] for i in place])


def joined_states(held, orders, logs, forward):
    count, mine = logs.shape[0], lax.axis_index("seq")
    who = jnp.arange(count) ^ mine
    if forward:
        counts = who < mine
        between = (who[None] > who[:, None]) & (who[None] < mine)
    else:
        counts = who > mine
        between = (who[None] < who[:, None]) & (who[None] > mine)
    power = jnp.sum(jnp.where(between[:, :, None], logs[None], 0.0), axis=1)
    factor = jnp.where(counts[:, None], jnp.exp2(power), 0.0)
    factor = jnp.repeat(factor[:, :H], P_SIZE, axis=1)
    half = E // 2
    sides = []
    for side in range(2):
        total = 0.0
        for i, k in enumerate(orders[side]):
            weight = factor[k, side * half : (side + 1) * half]
            total = total + weight[None] * held[side][i, :N].astype(f32)
        sides.append(total)
    return jnp.concatenate(sides, axis=1)


def cut(value, width, side):
    return lax.dynamic_slice_in_dim(value, side * width, width, 1)


def gathered(piece):
    return lax.all_gather(piece, "fsdp", axis=0, tiled=True)


def both_cores(mine):
    return mine, swapped(mine, "seq", 1)


def far_product(left, right, width, core):
    return tn(left, cut(right, width, 1 - core)).astype(bf16)


def half_product(left, right, width, core, came):
    return (tn(left, cut(right, width, core)) + came.astype(f32)).astype(bf16)


def part_sum(value):
    return lax.psum_scatter(value, "fsdp", scatter_dimension=0, tiled=True)


def added(value, bit):
    return (value.astype(f32) + swapped(value, "seq", bit).astype(f32)).astype(bf16)


def plane_step(first, second, k):
    bits = bits_of("seq")[1:]
    return added(first, bits[k]), added(second, bits[-1 - k])


def plane_sum(first, second):
    for k in range(len(bits_of("seq")) - 1):
        first, second = plane_step(first, second, k)
    return first, second


def swapped_pair(value):
    return value, swapped(value, "seq", 1)


def big_of(mine, other, core):
    def both(low, high):
        return ordered(mine[:, low:high], other[:, low:high], core)

    at = HZ + 2 * HD
    gate, conv = both(0, HZ), both(at, at + HX)
    tops, bottoms = both(HZ, HZ + HD), both(HZ + HD, at)
    steps = mine[:, at + HX : at + HX + H]
    return (
        jnp.concatenate([gate, conv, steps], axis=1).astype(f32),
        jnp.concatenate([tops, bottoms]).astype(f32),
    )


def plane_sum_rows(value):
    half = value.shape[0] // 2
    return jnp.concatenate(plane_sum(value[:half], value[half:]))


def ordered(mine, other, core):
    return jnp.concatenate(
        [jnp.where(core == 0, mine, other), jnp.where(core == 0, other, mine)], axis=1
    )


def reduced_small(value):
    parts, mine = lax.axis_size("fsdp"), lax.axis_index("fsdp")
    bit = parts // 2
    while bit:
        value = value.reshape((2, value.shape[0] // 2) + value.shape[1:])
        upper = (mine & bit) != 0
        kept = jnp.where(upper, value[1], value[0])
        value = kept + swapped(jnp.where(upper, value[0], value[1]), "fsdp", bit)
        bit //= 2
    for bit in bits_of("seq"):
        value = value + swapped(value, "seq", bit)
    return value[0]


def pad_lanes(value):
    return jnp.pad(value, ((0, 0), (0, 128 - value.shape[1])))


def token_table(doc, edge_ids):
    t = doc.shape[0]
    widened = jnp.concatenate([edge_ids, doc, jnp.full((K - 1,), -1, doc.dtype)])
    ids = [widened[k : k + t] == doc for k in range(K - 1)]
    ids += [widened[K - 1 + (K - 1 - k) :][:t] == doc for k in range(K - 1)]
    before = widened[K - 2 : K - 2 + t].reshape(t // Q, Q)[:, :1]
    blocks = doc.reshape(t // Q, Q)
    ids.append((blocks == before).reshape(t))
    ids.append((blocks == blocks[:, Q - 1 :]).reshape(t))
    cols_in = [v.astype(f32) for v in ids] + [doc.astype(f32)]
    table = pad_lanes(jnp.stack(cols_in, axis=1))
    return table, jnp.broadcast_to(doc.astype(f32)[None], (8, t))


def constants():
    spread = np.zeros((128, E), np.float32)
    for h in range(H):
        spread[h, h * P_SIZE : (h + 1) * P_SIZE] = 1
    hot = np.zeros((PAIRS, 2 * Q, 128), np.float32)
    sel = np.zeros((PAIRS, HP, 2 * Q), np.float32)
    for p in range(PAIRS):
        for i in range(2):
            hot[p, i * Q : (i + 1) * Q, 2 * p + i] = 1
            sel[p, 2 * p + i, i * Q : (i + 1) * Q] = 1
    return tuple(
        jnp.asarray(v, bf16) for v in (np.concatenate([spread, spread]), spread.T, hot, sel)
    )


SMALL = (K * CV, CV, H, H, H, D, E)


def local(
    first_tier_source,
    token_articles,
    extra_spikes,
    upstream_gradient,
    entering_projection,
    exit_projection,
    filter_kernels,
    filter_shifts,
    stride_shifts,
    log_shrink_rates,
    bypass_coefficient,
    entry_scaling_gains,
    gated_scaling_gains,
):
    current = first_tier_source[0]
    doc = token_articles[0]
    spike = pad_lanes(extra_spikes[0])
    t = doc.shape[0]
    layers = entering_projection.shape[0]
    parts = lax.axis_size("fsdp")
    e2, et, hot, sel = constants()
    edge_ids = passed_along(doc[t - (K - 1) :], "seq", 1)
    tok, doct = token_table(doc, edge_ids)

    small = (
        filter_kernels, filter_shifts, stride_shifts, log_shrink_rates, bypass_coefficient,
        entry_scaling_gains, gated_scaling_gains,
    )
    flat = jnp.concatenate([v.reshape(layers, -1) for v in small], axis=1)
    flat = lax.all_gather(flat, "fsdp").astype(f32)

    def small_of(layer):
        found, at = [], 0
        for size in SMALL:
            width = size // parts
            found.append(flat[:, layer, at : at + width])
            at += width
        taps = found[0].reshape(parts, K, CV // parts).transpose(1, 0, 2).reshape(K, CV)
        return [taps] + [v.reshape(-1) for v in found[1:]]

    core = lax.axis_index("seq") & 1
    cores = jnp.reshape(core, (1,)).astype(jnp.int32)
    bits = bits_of("seq")
    found = []
    for i in range(layers):
        w = entering_projection[i]
        steps = jnp.pad(w[:, E + CV :], ((0, 0), (0, 128 - H)))
        piece = jnp.concatenate([cut(w[:, E : E + CV], HX, core), steps], axis=1)
        gate, out = cut(w[:, :E], HZ, core), cut(exit_projection[i], HD, core)
        if i == 0:
            found.append((gathered(piece), gathered(gate), gathered(out)))
        else:
            rest = out.shape[0] // 2
            both = gathered(jnp.concatenate([gate, out[:rest], out[rest:]], axis=1))
            found.append((gathered(piece), both, None))
    weights = []
    kept = []
    for i in range(layers):
        wx = found[i][0]
        wx = both_cores(wx if i == 0 else tied(wx, current))
        taps, shifts, strides, rates, bypass, gain_in, gain_out = small_of(i)
        cw = jnp.concatenate([taps, shifts[None], jnp.zeros((3, CV), f32)])
        pv = jnp.concatenate(
            [pad_lanes(jnp.stack([strides, jnp.exp(rates)])), jnp.zeros((6, 128), f32)]
        )
        skip = jnp.repeat(bypass, P_SIZE)[None]
        gain_in, gain_out = gain_in[None], gain_out[None]
        normed, xc, dtr = project(cores, current, gain_in, *wx)
        edge = passed_along(xc[t - (K - 1) :], "seq", 1).astype(f32)
        edge = jnp.concatenate([jnp.zeros((8 - (K - 1), CV), f32), edge])
        pre, x, bc, dt, cum, cumt, dtt, packed = prepare(xc, edge, cw, dtr, spike, tok, pv, e2)
        yi = within(x, bc, cum, cumt, dtt, tok, doct)
        if i == 0:
            wz = both_cores(tied(found[i][1], x))
            made = []

            def gate_beside(before):
                made.append(project_gate(cores, tied(normed, *before), *wz))
                return made[0]

            held, orders, stages = all_states(packed, lambda before: yi, gate_beside)
            wo, z = both_cores(tied(found[i][2], *stages[1])), made[0]
        else:
            held, orders, stages = all_states(packed, lambda before: yi)
            both = tied(found[i][1], *stages[1])
            wz, wo = both[:, :HZ], both[:, HZ:].reshape(parts, -1, 2, HD)
            wo = wo.transpose(0, 2, 1, 3).reshape(E, HD)
            wz, wo = both_cores(wz), both_cores(wo)
            z = project_gate(cores, tied(normed, *stages[0]), *wz)
        weights.append((wx, wz, wo))
        logs = decay_table(held[0], orders[0])
        incoming = joined_states(held, orders, logs, True)
        out_type = bf16 if i == layers - 1 else f32
        y, low, new, prior = across(
            cores, yi, x, bc, dt, cum, tok, z, incoming, skip, gain_out, *wo, current, e2, out_type
        )
        kept.append(
            (current, normed, z, xc, dtr, edge, pre, x, bc, dt, cum, cumt, logs, y, low, prior,
             cw, pv, skip, gain_in, gain_out)
        )
        current = new
    grad = upstream_gradient[0]
    results = [None] * layers
    waiting = {}
    for i in reversed(range(layers)):
        wx, wz, wo = weights[i]
        (source, normed, z, xc, dtr, edge, pre, x, bc, dt, cum, cumt, logs, y, low, prior,
         cw, pv, skip, gain_in, gain_out) = kept[i]
        dy, dz, gb, acc, state = open_back(
            cores, grad, *wo, y, z, x, bc, cum, tok, gain_out, e2
        )
        far_gate = far_product(normed, dz, HZ, core)
        far_out = far_product(low, gb, HD, core)
        shared = (bc, dt, cum, cumt, tok, doct, hot, sel)
        near0 = within_back(tied(x, far_gate, far_out), dy, *shared, 0)
        top = waiting.get(i + 1)
        near1 = []

        def second_half(before):
            near1.extend(within_back(tied(x, near0[2], *before), dy, *shared, 1))
            return near1[2]

        came = (swapped(far_gate, "seq", 1), swapped(far_out, "seq", 1))
        held, orders, stages = all_states(state, lambda before: (near0[2], came), second_half)
        half_gate = half_product(normed, tied(dz, near1[2]), HZ, core, came[0])
        half_out = half_product(low, tied(gb, near1[2]), HD, core, came[1])
        grad_out, grad_gate = part_sum(half_out), part_sum(half_gate)
        later = joined_states(held, orders, logs, False)
        later = tied(later, half_out, half_gate)
        if top is not None:
            sums = added(tied(top, later), bits[1])
        dxc, cacc, hacc, first = across_back(
            x, pre, xc, edge, bc, dy, near0, near1, dt, cum, dtr, tok, prior, later, skip, cw, pv, e2, et
        )
        if top is not None:
            first, sums = together(first, sums)
        first, grad_out = together(first, grad_out)
        masked = [first[: K - 1] * tok[: K - 1, k : k + 1] for k in range(K - 1)]
        borrowed = jnp.stack(
            [sum(cw[k] * masked[k][e - k] for k in range(e + 1)) for e in range(K - 1)]
        )
        back = passed_along(borrowed, "seq", -1)
        gap = jnp.zeros((K - 1, 128), f32)
        back = jnp.concatenate([back[:, :HX], gap, back[:, HX:], gap], axis=1)
        mended = (dxc[t - (K - 1) :].astype(f32) + back).astype(bf16)
        dxc = dxc.at[t - (K - 1) :].set(mended)
        dxc, grad_gate = together(dxc, grad_gate)
        far_conv = far_product(normed, dxc, CX, core)
        conv_half = half_product(normed, dxc, CX, core, swapped(far_conv, "seq", 1))
        rest = grad_out.shape[0] // 2
        grad_out = jnp.concatenate([grad_out[:rest], grad_out[rest:]], axis=1)
        if i == 0:
            early = plane_sum(*tied((grad_gate, grad_out), far_conv))
            if top is not None:
                for bit in bits[2:]:
                    sums = added(sums, bit)
                grad = tied(grad, sums)
                results[i + 1] += (swapped_pair(sums),)
            grad = tied(grad, conv_half, *early)
            early = swapped_pair(jnp.concatenate(early, axis=1))
        grad, nacc = close_back(cores, dz, dxc, wz, wx, source, gain_in, grad)
        grad_conv = part_sum(conv_half)
        if i > 0:
            grad = tied(grad, conv_half)
            waiting[i] = jnp.concatenate([grad_gate, grad_out, grad_conv], axis=1)
        tiny = [
            cacc[:K], cacc[K], hacc[0, :H], hacc[1, :H],
            jnp.sum(acc[1].reshape(H, P_SIZE), axis=1), nacc[0], acc[0],
        ]
        results[i] = (tiny,)
    packed = []
    for i in range(layers):
        tiny = results[i][0]
        taps = tiny[0].reshape(K, parts, CV // parts).transpose(1, 0, 2).reshape(parts, -1)
        packed.append(jnp.concatenate([taps] + [v.reshape(parts, -1) for v in tiny[1:]], axis=1))
    mine = reduced_small(tied(jnp.stack(packed, axis=1), grad_conv))
    late = swapped_pair(plane_sum_rows(grad_conv))
    results[0] += (tuple(jnp.concatenate(v, axis=1) for v in zip(early, late)),)
    bigs = [
        big_of(*(tied(results[i][1], grad_conv) if i else results[i][1]), core)
        for i in range(layers)
    ]
    smalls, at = [], 0
    for size in SMALL:
        width = size // parts
        smalls.append(mine[:, at : at + width])
        at += width
    smalls[0] = smalls[0].reshape(layers, K, CV // parts)
    bigs = [jnp.stack([v[j] for v in bigs]) for j in range(2)]
    return (current[None], grad[None], *bigs, *smalls)


def solution(mesh):
    placed = (
        P("fsdp", "seq", None),
        P("fsdp", "seq"),
        P("fsdp", "seq", None),
        P("fsdp", "seq", None),
        P(None, "fsdp", None),
        P(None, "fsdp", None),
        P(None, None, "fsdp"),
        P(None, "fsdp"),
        P(None, "fsdp"),
        P(None, "fsdp"),
        P(None, "fsdp"),
        P(None, "fsdp"),
        P(None, "fsdp"),
    )
    return jax.shard_map(
        local,
        mesh=mesh,
        in_specs=placed,
        out_specs=(
            P("fsdp", "seq", None),
            P("fsdp", "seq", None),
            P(None, "fsdp", None),
            P(None, "fsdp", None),
            P(None, None, "fsdp"),
            P(None, "fsdp"),
            P(None, "fsdp"),
            P(None, "fsdp"),
            P(None, "fsdp"),
            P(None, "fsdp"),
            P(None, "fsdp"),
        ),
        check_vma=False,
    )
```

```python
from functools import partial

import jax
import jax.numpy as jnp
import numpy as np
from jax import lax
from jax.experimental import pallas as pl
from jax.experimental.pallas import tpu as pltpu
from jax.sharding import PartitionSpec as P

D = 768
H = 24
P_SIZE = 64
N = 128
K = 4
E = 1536
CV = 1792
HX = CV // 2
HZ = E // 2
HD = D // 2
CX = HX + 128
Q = 128
TT = 256
SUB = TT // Q
W = 256
HP = 32
PAIRS = H // 2
eps = 1e-05
LOG2E = 1.4426950408889634
BIG = -1e30
CUT = 30000.0
f32 = jnp.float32
bf16 = jnp.bfloat16
highest = lax.Precision.HIGHEST
VMEM_LIMIT = 56 * 1024 * 1024


def nn(a, b):
    return lax.dot_general(a, b, (((1,), (0,)), ((), ())), preferred_element_type=f32)


def nt(a, b):
    return lax.dot_general(a, b, (((1,), (1,)), ((), ())), preferred_element_type=f32)


def tn(a, b):
    return lax.dot_general(a, b, (((0,), (0,)), ((), ())), preferred_element_type=f32)


def nn_exact(a, b):
    return lax.dot_general(
        a, b, (((1,), (0,)), ((), ())), precision=highest, preferred_element_type=f32
    )


def halves(v):
    hi = v.astype(bf16)
    lo = (v - hi.astype(f32)).astype(bf16)
    return jnp.concatenate([hi, lo], axis=1)


def sigmoid(v):
    return 0.5 + 0.5 * jnp.tanh(0.5 * v)


def softplus(v):
    return jnp.maximum(v, 0.0) + jnp.log1p(jnp.exp(-jnp.abs(v)))


def iota2(shape, dim):
    return lax.broadcasted_iota(jnp.int32, shape, dim)


def lane_halves():
    lane = iota2((1, 2 * P_SIZE), 1)
    left = (lane < P_SIZE).astype(f32).astype(bf16)
    right = (lane >= P_SIZE).astype(f32).astype(bf16)
    return left, right


def full(shape):
    return pl.BlockSpec(shape, lambda i: (0,) * len(shape))


def rows(width, size=TT):
    return pl.BlockSpec((size, width), lambda i: (i, 0))


def cols(height):
    return pl.BlockSpec((height, TT), lambda i: (0, i))


def params():
    return pltpu.CompilerParams(vmem_limit_bytes=VMEM_LIMIT, dimension_semantics=("arbitrary",))


def cost(micros):
    return pl.CostEstimate(
        flops=int(micros * 1e9), bytes_accessed=int(micros * 3e6), transcendentals=0
    )


SMEM = pl.BlockSpec(memory_space=pltpu.SMEM)


def sides(core_ref, width):
    mine = core_ref[0] * width
    return pl.ds(pl.multiple_of(mine, 128), width), pl.ds(
        pl.multiple_of(width - mine, 128), width
    )


def shape(dims, dtype):
    return jax.ShapeDtypeStruct(dims, dtype)


def project_kernel(core_ref, x_ref, gain_ref, mine_ref, other_ref, normed_ref, xc_ref, dtr_ref):
    x = x_ref[...].astype(f32)
    scale = lax.rsqrt(jnp.mean(x * x, axis=-1, keepdims=True) + eps)
    normed = (x * scale * gain_ref[...]).astype(bf16)
    normed_ref[...] = normed
    own, far = sides(core_ref, HX)
    xc_ref[:, own] = nn(normed, mine_ref[:, :HX]).astype(bf16)
    dtr_ref[...] = nn(normed, mine_ref[:, HX:])
    xc_ref[:, far] = nn(normed, other_ref[:, :HX]).astype(bf16)


def project(core, x, gain, mine, other):
    t = x.shape[0]
    return pl.pallas_call(
        project_kernel,
        grid=(t // TT,),
        in_specs=[SMEM, rows(D), full((1, D)), full((D, CX)), full((D, CX))],
        out_specs=[rows(D), rows(CV), rows(128)],
        out_shape=[shape((t, D), bf16), shape((t, CV), bf16), shape((t, 128), f32)],
        compiler_params=params(),
        cost_estimate=cost(8),
        name="project",
    )(core, x, gain, mine, other)


def gate_kernel(core_ref, normed_ref, mine_ref, other_ref, z_ref):
    own, far = sides(core_ref, HZ)
    z_ref[:, own] = nn(normed_ref[...], mine_ref[...]).astype(bf16)
    z_ref[:, far] = nn(normed_ref[...], other_ref[...]).astype(bf16)


def project_gate(core, normed, mine, other):
    t = normed.shape[0]
    return pl.pallas_call(
        gate_kernel,
        grid=(t // TT,),
        in_specs=[SMEM, rows(D), full((D, HZ)), full((D, HZ))],
        out_specs=rows(E),
        out_shape=shape((t, E), bf16),
        compiler_params=params(),
        cost_estimate=cost(6),
        name="project_gate",
    )(core, normed, mine, other)


def prepare_kernel(
    xc_ref, edge_ref, cw_ref, dtr_ref, spike_ref, tok_ref, pv_ref, e2_ref,
    pre_ref, x_ref, bc_ref, dt_ref, cum_ref, cumt_ref, dtt_ref, packed_ref,
    ext, state_ref, carry_ref,
):
    step = pl.program_id(0)

    @pl.when(step == 0)
    def _():
        ext[0:8, :] = edge_ref[...]
        state_ref[...] = jnp.zeros_like(state_ref)
        carry_ref[...] = jnp.zeros_like(carry_ref)

    @pl.when(step > 0)
    def _():
        ext[0:8, :] = ext[TT : TT + 8, :]

    ext[8 : TT + 8, :] = xc_ref[...].astype(f32)
    masks = [tok_ref[:, k : k + 1] for k in range(K - 1)]
    for b in range(CV // 128):
        at = slice(b * 128, (b + 1) * 128)
        total = cw_ref[K : K + 1, at] + cw_ref[K - 1 : K, at] * ext[8 : TT + 8, at]
        for k in range(K - 1):
            total = total + cw_ref[k : k + 1, at] * (ext[5 + k : 5 + k + TT, at] * masks[k])
        pre_ref[:, at] = total.astype(bf16)
        act = (total * sigmoid(total)).astype(bf16)
        if b < E // 128:
            x_ref[:, at] = act
        else:
            bc_ref[:, (b - E // 128) * 128 : (b - E // 128 + 1) * 128] = act

    dt = softplus(dtr_ref[...] + pv_ref[0:1, :])
    log_decay = (spike_ref[...] - dt * pv_ref[1:2, :]) * LOG2E
    dt_ref[...] = dt
    dtt_ref[...] = jnp.transpose(dt)[:HP, :]
    lower = (iota2((Q, Q), 0) >= iota2((Q, Q), 1)).astype(f32)
    for s in range(SUB):
        r = slice(s * Q, (s + 1) * Q)
        cum = nn_exact(lower, log_decay[r])
        cum_ref[r, :] = cum
        cumt_ref[:, r] = jnp.transpose(cum)[:HP, :]
        last = cum[Q - 1 : Q, :]
        tail = jnp.exp2(last - cum) * tok_ref[r, 7:8] * dt[r]
        kept = tok_ref[s * Q + Q - 1 : s * Q + Q, 6:7]
        carried = jnp.exp2(last) * kept
        carry_ref[...] = carry_ref[...] + (last + (kept - 1.0) * CUT)
        wide = jnp.concatenate([tail, jnp.broadcast_to(carried, (16, 128))], axis=0)
        wide = halves(wide)
        b_in = bc_ref[r, :N]
        for b in range(E // W):
            at = slice(b * W, (b + 1) * W)
            grown = nn(wide, e2_ref[:, at])
            weighted = (x_ref[r, at].astype(f32) * grown[:Q]).astype(bf16)
            state_ref[:, at] = state_ref[:, at] * grown[Q : Q + 1] + tn(b_in, weighted)

    @pl.when(step == pl.num_programs(0) - 1)
    def _():
        packed_ref[:N, :] = state_ref[...].astype(bf16)
        packed_ref[N:, :] = jnp.zeros((16, E), bf16)
        rest = jnp.concatenate([carry_ref[...], carry_ref[...]], axis=0)
        for k in range(3):
            part = rest.astype(bf16)
            packed_ref[N:, k * 128 : (k + 1) * 128] = part
            rest = rest - part.astype(f32)


def prepare(xc, edge, cw, dtr, spike, tok, pv, e2):
    t = xc.shape[0]
    return pl.pallas_call(
        prepare_kernel,
        grid=(t // TT,),
        in_specs=[
            rows(CV), full((8, CV)), full((8, CV)), rows(128), rows(128), rows(128),
            full((8, 128)), full((256, E)),
        ],
        out_specs=[
            rows(CV), rows(E), rows(2 * N), rows(128), rows(128), cols(HP), cols(HP),
            full((N + 16, E)),
        ],
        out_shape=[
            shape((t, CV), bf16),
            shape((t, E), bf16),
            shape((t, 2 * N), bf16),
            shape((t, 128), f32),
            shape((t, 128), f32),
            shape((HP, t), f32),
            shape((HP, t), f32),
            shape((N + 16, E), bf16),
        ],
        scratch_shapes=[
            pltpu.VMEM((TT + 8, CV), f32),
            pltpu.VMEM((N, E), f32),
            pltpu.VMEM((8, 128), f32),
        ],
        compiler_params=params(),
        cost_estimate=cost(15),
        name="prepare",
    )(xc, edge, cw, dtr, spike, tok, pv, e2)


def within_kernel(x_ref, bc_ref, cum_ref, cumt_ref, dtt_ref, tok_ref, doct_ref, y_ref):
    left, right = lane_halves()
    order = iota2((Q, Q), 0) >= iota2((Q, Q), 1)
    for s in range(SUB):
        r = slice(s * Q, (s + 1) * Q)
        same = tok_ref[r, 8:9] == doct_ref[0:1, r]
        bias = jnp.where(order & same, 0.0, BIG)
        scores = nt(bc_ref[r, N:], bc_ref[r, :N])
        cum = cum_ref[r, :]
        for p in range(PAIRS):
            at = slice(p * 128, (p + 1) * 128)
            xp = x_ref[r, at]
            mixes = []
            for h in (2 * p, 2 * p + 1):
                gap = (cum[:, h : h + 1] - cumt_ref[h : h + 1, r]) + bias
                mixes.append((jnp.exp2(gap) * (scores * dtt_ref[h : h + 1, r])).astype(bf16))
            both = jnp.concatenate([xp * left, xp * right], axis=0)
            y_ref[r, at] = nn(jnp.concatenate(mixes, axis=1), both).astype(bf16)


def within(x, bc, cum, cumt, dtt, tok, doct):
    t = x.shape[0]
    return pl.pallas_call(
        within_kernel,
        grid=(t // TT,),
        in_specs=[rows(E), rows(2 * N), rows(128), cols(HP), cols(HP), rows(128), cols(8)],
        out_specs=rows(E),
        out_shape=shape((t, E), bf16),
        compiler_params=params(),
        cost_estimate=cost(8),
        name="within",
    )(x, bc, cum, cumt, dtt, tok, doct)


def across_kernel(
    core_ref, yi_ref, x_ref, bc_ref, dt_ref, cum_ref, tok_ref, z_ref, first_ref, skip_ref,
    gain_ref, mine_ref, other_ref, res_ref, e2_ref,
    y_ref, low_ref, new_ref, prior_ref,
    state, gated,
):
    step = pl.program_id(0)

    @pl.when(step == 0)
    def _():
        state[...] = first_ref[...]

    for s in range(SUB):
        r = slice(s * Q, (s + 1) * Q)
        cum = cum_ref[r, :]
        last = cum[Q - 1 : Q, :]
        tail = jnp.exp2(last - cum) * tok_ref[r, 7:8] * dt_ref[r, :]
        head = jnp.exp2(cum) * tok_ref[r, 6:7]
        carried = head[Q - 1 : Q, :]
        wide = halves(
            jnp.concatenate([tail, head, jnp.broadcast_to(carried, (16, 128))], axis=0)
        )
        b_in = bc_ref[r, :N]
        c_out = bc_ref[r, N:]
        square = jnp.zeros((Q, W), f32)
        for b in range(E // W):
            at = slice(b * W, (b + 1) * W)
            grown = nn(wide, e2_ref[:, at])
            xs = x_ref[r, at].astype(f32)
            held = state[:, at]
            prior_ref[s, :, at] = held.astype(bf16)
            y = (
                yi_ref[r, at].astype(f32)
                + nn(c_out, held.astype(bf16)) * grown[Q : 2 * Q]
                + skip_ref[0:1, at] * xs
            )
            y_ref[r, at] = y.astype(bf16)
            z = z_ref[r, at].astype(f32)
            made = y * (z * sigmoid(z))
            gated[r, at] = made
            square = square + made * made
            weighted = (xs * grown[:Q]).astype(bf16)
            state[:, at] = held * grown[2 * Q : 2 * Q + 1] + tn(b_in, weighted)
        scale = lax.rsqrt(jnp.sum(square, axis=-1, keepdims=True) * (1.0 / E) + eps)
        for b in range(E // W):
            at = slice(b * W, (b + 1) * W)
            low_ref[r, at] = (gated[r, at] * scale * gain_ref[0:1, at]).astype(bf16)
    for at, w_ref in zip(sides(core_ref, HD), (mine_ref, other_ref)):
        new = res_ref[:, at].astype(f32) + nn(low_ref[...], w_ref[...])
        new_ref[:, at] = new.astype(new_ref.dtype)


def across(core, yi, x, bc, dt, cum, tok, z, first, skip, gain, mine, other, res, e2, out_type):
    t = x.shape[0]
    return pl.pallas_call(
        across_kernel,
        grid=(t // TT,),
        in_specs=[
            SMEM, rows(E), rows(E), rows(2 * N), rows(128), rows(128), rows(128), rows(E),
            full((N, E)), full((1, E)), full((1, E)), full((E, HD)), full((E, HD)), rows(D),
            full((256, E)),
        ],
        out_specs=[rows(E), rows(E), rows(D), pl.BlockSpec((SUB, N, E), lambda i: (i, 0, 0))],
        out_shape=[
            shape((t, E), bf16),
            shape((t, E), bf16),
            shape((t, D), out_type),
            shape((t // Q, N, E), bf16),
        ],
        scratch_shapes=[pltpu.VMEM((N, E), f32), pltpu.VMEM((TT, E), f32)],
        compiler_params=params(),
        cost_estimate=cost(16),
        name="across",
    )(core, yi, x, bc, dt, cum, tok, z, first, skip, gain, mine, other, res, e2)


def open_back_kernel(
    core_ref, g_ref, mine_ref, other_ref, y_ref, z_ref, x_ref, bc_ref, cum_ref, tok_ref,
    gain_ref, e2_ref,
    dy_ref, dz_ref, gb_ref, acc_ref, low_ref,
    held, state_ref,
):
    step = pl.program_id(0)

    @pl.when(step == 0)
    def _():
        acc_ref[...] = jnp.zeros_like(acc_ref)
        state_ref[...] = jnp.zeros_like(state_ref)

    gb_ref[...] = g_ref[...].astype(bf16)
    own, far = sides(core_ref, HD)
    held[...] = nt(gb_ref[:, own], mine_ref[...]) + nt(gb_ref[:, far], other_ref[...])
    for s in reversed(range(SUB)):
        r = slice(s * Q, (s + 1) * Q)
        square = jnp.zeros((Q, W), f32)
        cross = jnp.zeros((Q, W), f32)
        for b in range(E // W):
            at = slice(b * W, (b + 1) * W)
            z = z_ref[r, at].astype(f32)
            gated = y_ref[r, at].astype(f32) * (z * sigmoid(z))
            square = square + gated * gated
            cross = cross + gated * (held[r, at] * gain_ref[0:1, at])
        scale = lax.rsqrt(jnp.sum(square, axis=-1, keepdims=True) * (1.0 / E) + eps)
        pull = (scale * scale * scale) * (jnp.sum(cross, axis=-1, keepdims=True) * (1.0 / E))
        cum = cum_ref[r, :]
        head = jnp.exp2(cum) * tok_ref[r, 6:7]
        wide = halves(
            jnp.concatenate([head, jnp.broadcast_to(head[Q - 1 : Q, :], (16, 128))], axis=0)
        )
        c_out = bc_ref[r, N:]
        for b in range(E // W):
            at = slice(b * W, (b + 1) * W)
            z = z_ref[r, at].astype(f32)
            gate = sigmoid(z)
            y = y_ref[r, at].astype(f32)
            gated = y * (z * gate)
            dn = held[r, at]
            acc_ref[0:1, at] += jnp.sum(dn * (gated * scale), axis=0, keepdims=True)
            dgated = scale * (dn * gain_ref[0:1, at]) - gated * pull
            dy = dgated * (z * gate)
            dz_ref[r, at] = (dgated * y * (gate * (1.0 + z * (1.0 - gate)))).astype(bf16)
            acc_ref[1:2, at] += jnp.sum(dy * x_ref[r, at].astype(f32), axis=0, keepdims=True)
            dy_ref[r, at] = dy.astype(bf16)
            grown = nn(wide, e2_ref[:, at])
            state_ref[:, at] = state_ref[:, at] * grown[Q : Q + 1] + tn(
                c_out, (dy * grown[:Q]).astype(bf16)
            )

    @pl.when(step == pl.num_programs(0) - 1)
    def _():
        low_ref[...] = state_ref[...].astype(bf16)


def open_back(core, g, mine, other, y, z, x, bc, cum, tok, gain, e2):
    t = x.shape[0]
    n = t // TT

    def turned(width):
        return pl.BlockSpec((TT, width), lambda i: (n - 1 - i, 0))

    return pl.pallas_call(
        open_back_kernel,
        grid=(n,),
        in_specs=[
            SMEM, turned(D), full((E, HD)), full((E, HD)), turned(E), turned(E), turned(E),
            turned(2 * N), turned(128), turned(128), full((1, E)), full((256, E)),
        ],
        out_specs=[turned(E), turned(E), turned(D), full((8, E)), full((N, E))],
        out_shape=[
            shape((t, E), bf16),
            shape((t, E), bf16),
            shape((t, D), bf16),
            shape((8, E), f32),
            shape((N, E), bf16),
        ],
        scratch_shapes=[pltpu.VMEM((TT, E), f32), pltpu.VMEM((N, E), f32)],
        compiler_params=params(),
        cost_estimate=cost(20),
        name="open_back",
    )(core, g, mine, other, y, z, x, bc, cum, tok, gain, e2)


def within_back_kernel(
    pairs,
    x_ref, dy_ref, bc_ref, dt_ref, cum_ref, cumt_ref, tok_ref, doct_ref, hot_ref, sel_ref,
    dxdt_ref, dbc_ref, cross_ref,
):
    left, right = lane_halves()
    order = iota2((Q, Q), 1) >= iota2((Q, Q), 0)
    suffix = order.astype(f32)
    for s in range(SUB):
        r = slice(s * Q, (s + 1) * Q)
        same = tok_ref[r, 8:9] == doct_ref[0:1, r]
        bias = jnp.where(order & same, 0.0, BIG)
        b_in = bc_ref[r, :N]
        c_out = bc_ref[r, N:]
        scores = nt(b_in, c_out)
        cum = cum_ref[r, :]
        dt = dt_ref[r, :]
        grad_scores = jnp.zeros((Q, Q), f32)
        by_source = jnp.zeros((Q, 128), f32)
        by_target = jnp.zeros((HP, Q), f32)
        for p in pairs:
            at = slice((p - pairs[0]) * 128, (p - pairs[0] + 1) * 128)
            xp = x_ref[r, at]
            dyp = dy_ref[r, at]
            dmix = nt(jnp.concatenate([xp * left, xp * right], axis=0), dyp)
            mixes = []
            flows = []
            for i in range(2):
                h = 2 * p + i
                decay = jnp.exp2((cumt_ref[h : h + 1, r] - cum[:, h : h + 1]) + bias)
                mixes.append((decay * scores).astype(bf16))
                part = dmix[i * Q : (i + 1) * Q] * (decay * dt[:, h : h + 1])
                grad_scores = grad_scores + part
                flows.append((part * scores).astype(bf16))
            both = jnp.concatenate([dyp * left, dyp * right], axis=0)
            dxdt_ref[r, at] = nn(jnp.concatenate(mixes, axis=1), both).astype(bf16)
            by_source = by_source + nn(
                jnp.concatenate(flows, axis=1), hot_ref[p - pairs[0]]
            )
            by_target = by_target + nn(
                sel_ref[p - pairs[0]], jnp.concatenate(flows, axis=0)
            )
        low = grad_scores.astype(bf16)
        dbc_ref[r, :N] = nn(low, c_out)
        dbc_ref[r, N:] = tn(low, b_in)
        target = jnp.transpose(
            jnp.concatenate([by_target, jnp.zeros((128 - HP, Q), f32)], axis=0)
        )
        cross_ref[r, :] = nn_exact(suffix, target - by_source)


def within_back(x, dy, bc, dt, cum, cumt, tok, doct, hot, sel, part):
    t = x.shape[0]
    size = PAIRS // 2
    half = pl.BlockSpec((TT, HZ), lambda i: (i, part))
    return pl.pallas_call(
        partial(within_back_kernel, range(part * size, (part + 1) * size)),
        grid=(t // TT,),
        in_specs=[
            half, half, rows(2 * N), rows(128), rows(128), cols(HP), rows(128), cols(8),
            pl.BlockSpec((size,) + hot.shape[1:], lambda i: (part, 0, 0)),
            pl.BlockSpec((size,) + sel.shape[1:], lambda i: (part, 0, 0)),
        ],
        out_specs=[rows(HZ), rows(2 * N), rows(128)],
        out_shape=[shape((t, HZ), bf16), shape((t, 2 * N), f32), shape((t, 128), f32)],
        compiler_params=params(),
        cost_estimate=cost(12),
        name="within_back",
    )(x, dy, bc, dt, cum, cumt, tok, doct, hot, sel)


def across_back_kernel(
    x_ref, pre_ref, xc_ref, halo_ref, edge_ref, bc_ref, dy_ref, dxdt0_ref, dxdt1_ref,
    dbc0_ref, dbc1_ref, cross0_ref, cross1_ref,
    dt_ref, cum_ref, dtr_ref, tok_ref, prior_ref, last_ref, skip_ref, cw_ref, pv_ref, e2_ref,
    et_ref,
    dxc_ref, cacc_ref, hacc_ref, first_ref,
    state, dp, ext,
):
    step = pl.program_id(0)
    count = pl.num_programs(0)

    @pl.when(step == 0)
    def _():
        state[...] = last_ref[...]
        cacc_ref[...] = jnp.zeros_like(cacc_ref)
        hacc_ref[...] = jnp.zeros_like(hacc_ref)
        dp[TT : TT + 8, :] = jnp.zeros((8, CV), f32)

    @pl.when(step > 0)
    def _():
        dp[TT : TT + 8, :] = dp[0:8, :]

    @pl.when(step == count - 1)
    def _():
        ext[0:8, :] = edge_ref[...]

    @pl.when(step < count - 1)
    def _():
        ext[0:8, :] = halo_ref[...].astype(f32)[8:16, :]

    def through_silu(grad, r, at):
        v = pre_ref[r, at].astype(f32)
        gate = sigmoid(v)
        dp[r, at] = grad * (gate * (1.0 + v * (1.0 - gate)))

    strict = (iota2((Q, Q), 0) > iota2((Q, Q), 1)).astype(f32)
    suffix = (iota2((Q, Q), 0) <= iota2((Q, Q), 1)).astype(f32)
    rate = pv_ref[1:2, :]
    for s in reversed(range(SUB)):
        r = slice(s * Q, (s + 1) * Q)
        cum = cum_ref[r, :]
        dt = dt_ref[r, :]
        last = cum[Q - 1 : Q, :]
        tail = jnp.exp2(last - cum) * tok_ref[r, 7:8]
        head = jnp.exp2(cum) * tok_ref[r, 6:7]
        carried = head[Q - 1 : Q, :]
        wide = halves(
            jnp.concatenate([tail, head, dt, jnp.broadcast_to(carried, (16, 128))], axis=0)
        )
        b_in = bc_ref[r, :N]
        c_out = bc_ref[r, N:]
        grad_b = dbc0_ref[r, :N] + dbc1_ref[r, :N]
        grad_c = dbc0_ref[r, N:] + dbc1_ref[r, N:]
        sums = jnp.zeros((3 * Q + 16, 128), f32)
        for b in range(E // W):
            at = slice(b * W, (b + 1) * W)
            grown = nn(wide, e2_ref[:, at])
            dt_wide = grown[2 * Q : 3 * Q]
            after = state[:, at]
            after_low = after.astype(bf16)
            before = prior_ref[s, :, at]
            xs = x_ref[r, at].astype(f32)
            dy = dy_ref[r, at].astype(f32)
            reach = nn(b_in, after_low) * grown[:Q]
            read = nn(c_out, before)
            near = (dxdt0_ref, dxdt1_ref)[b * W // HZ]
            dxdt = near[r, b * W % HZ : b * W % HZ + W].astype(f32) + reach
            dyg = dy * grown[Q : 2 * Q]
            dyg_low = dyg.astype(bf16)
            joint = jnp.sum(after * before.astype(f32), axis=0, keepdims=True)
            stacked = jnp.concatenate(
                [
                    (xs * dxdt).astype(bf16),
                    (xs * reach).astype(bf16),
                    (dyg * read).astype(bf16),
                    jnp.broadcast_to(joint, (16, W)).astype(bf16),
                ],
                axis=0,
            )
            sums = sums + nn(stacked, et_ref[at, :])
            through_silu(dxdt * dt_wide + skip_ref[0:1, at] * dy, r, at)
            grad_c = grad_c + nt(dyg_low, before)
            grad_b = grad_b + nt((xs * (grown[:Q] * dt_wide)).astype(bf16), after_low)
            state[:, at] = after * grown[3 * Q : 3 * Q + 1] + tn(c_out, dyg_low)
        through_silu(grad_b, r, slice(E, E + N))
        through_silu(grad_c, r, slice(E + N, CV))
        dlog = (
            cross0_ref[r, :]
            + cross1_ref[r, :]
            + nn_exact(strict, sums[Q : 2 * Q] * dt)
            + nn_exact(suffix, sums[2 * Q : 3 * Q])
            + carried * sums[3 * Q : 3 * Q + 1]
        )
        draw = (sums[:Q] - rate * dlog) * sigmoid(dtr_ref[r, :] + pv_ref[0:1, :])
        dxc_ref[r, HX:CX] = draw.astype(bf16)
        dxc_ref[r, CX + HX :] = draw.astype(bf16)
        hacc_ref[0:1, :] += jnp.sum(draw, axis=0, keepdims=True)
        hacc_ref[1:2, :] -= rate * jnp.sum(dt * dlog, axis=0, keepdims=True)

    ext[8 : TT + 8, :] = xc_ref[...].astype(f32)
    masks = [tok_ref[:, k : k + 1] for k in range(K - 1)]
    ahead = [tok_ref[:, 3 + k : 4 + k] for k in range(K - 1)]
    for b in range(CV // 128):
        at = slice(b * 128, (b + 1) * 128)
        own = dp[0:TT, at]
        total = cw_ref[K - 1 : K, at] * own
        cacc_ref[K : K + 1, at] += jnp.sum(own, axis=0, keepdims=True)
        cacc_ref[K - 1 : K, at] += jnp.sum(own * ext[8 : TT + 8, at], axis=0, keepdims=True)
        for k in range(K - 1):
            total = total + cw_ref[k : k + 1, at] * (dp[3 - k : 3 - k + TT, at] * ahead[k])
            cacc_ref[k : k + 1, at] += jnp.sum(
                own * (ext[5 + k : 5 + k + TT, at] * masks[k]), axis=0, keepdims=True
            )
        to = b * 128 + (128 if b * 128 >= HX else 0)
        dxc_ref[:, to : to + 128] = total.astype(bf16)

    @pl.when(step == count - 1)
    def _():
        first_ref[...] = dp[0:8, :]


def across_back(
    x, pre, xc, edge, bc, dy, near0, near1, dt, cum, dtr, tok, prior, last, skip, cw, pv, e2, et
):
    t = x.shape[0]
    n = t // TT

    def turned(width):
        return pl.BlockSpec((TT, width), lambda i: (n - 1 - i, 0))

    halo = pl.BlockSpec((16, CV), lambda i: (jnp.maximum((n - 1 - i) * (TT // 16) - 1, 0), 0))
    return pl.pallas_call(
        across_back_kernel,
        grid=(n,),
        in_specs=[
            turned(E), turned(CV), turned(CV), halo, full((8, CV)), turned(2 * N), turned(E),
            turned(HZ), turned(HZ), turned(2 * N), turned(2 * N), turned(128), turned(128),
            turned(128), turned(128), turned(128), turned(128), pl.BlockSpec((SUB, N, E), lambda i: (n - 1 - i, 0, 0)), full((N, E)),
            full((1, E)), full((8, CV)), full((8, 128)), full((256, E)), full((E, 128)),
        ],
        out_specs=[turned(2 * CX), full((8, CV)), full((8, 128)), full((8, CV))],
        out_shape=[
            shape((t, 2 * CX), bf16),
            shape((8, CV), f32),
            shape((8, 128), f32),
            shape((8, CV), f32),
        ],
        scratch_shapes=[
            pltpu.VMEM((N, E), f32),
            pltpu.VMEM((TT + 8, CV), f32),
            pltpu.VMEM((TT + 8, CV), f32),
        ],
        compiler_params=params(),
        cost_estimate=cost(31),
        name="across_back",
    )(
        x, pre, xc, xc, edge, bc, dy, near0[0], near1[0], near0[1], near1[1], near0[2], near1[2],
        dt, cum, dtr, tok, prior, last, skip, cw, pv, e2, et,
    )


def close_back_kernel(
    core_ref, dz_ref, dxc_ref, zm_ref, zo_ref, xm_ref, xo_ref, x_ref, gain_ref, g_ref,
    new_ref, acc_ref,
):
    @pl.when(pl.program_id(0) == 0)
    def _():
        acc_ref[...] = jnp.zeros_like(acc_ref)

    own_z, far_z = sides(core_ref, HZ)
    own_x, far_x = sides(core_ref, CX)
    dn = (
        nt(dz_ref[:, own_z], zm_ref[...])
        + nt(dz_ref[:, far_z], zo_ref[...])
        + nt(dxc_ref[:, own_x], xm_ref[...])
        + nt(dxc_ref[:, far_x][:, :HX], xo_ref[:, :HX])
    )
    x = x_ref[...].astype(f32)
    scale = lax.rsqrt(jnp.mean(x * x, axis=-1, keepdims=True) + eps)
    acc_ref[0:1, :] += jnp.sum(dn * (x * scale), axis=0, keepdims=True)
    pulled = dn * gain_ref[...]
    mean = jnp.mean(pulled * x, axis=-1, keepdims=True)
    new_ref[...] = g_ref[...].astype(f32) + scale * pulled - x * (scale * scale * scale * mean)


def close_back(core, dz, dxc, zs, xs, x, gain, g):
    t = x.shape[0]
    return pl.pallas_call(
        close_back_kernel,
        grid=(t // TT,),
        in_specs=[
            SMEM, rows(E), rows(2 * CX), full((D, HZ)), full((D, HZ)), full((D, CX)),
            full((D, CX)), rows(D), full((1, D)), rows(D),
        ],
        out_specs=[rows(D), full((8, D))],
        out_shape=[shape((t, D), f32), shape((8, D), f32)],
        compiler_params=params(),
        cost_estimate=cost(12),
        name="close_back",
    )(core, dz, dxc, *zs, *xs, x, gain, g)


def passed_along(value, axis, steps):
    count = lax.axis_size(axis)
    first, last = (max(0, -steps), min(count, count - steps))
    return lax.ppermute(value, axis, [(source, source + steps) for source in range(first, last)])


def swapped(value, axis, bit):
    count = lax.axis_size(axis)
    return lax.ppermute(value, axis, [(source, source ^ bit) for source in range(count)])


def bits_of(axis):
    return [1 << k for k in range((lax.axis_size(axis) - 1).bit_length())]


def all_states(packed, *beside):
    bits = bits_of("seq")
    half = E // 2
    sides = [(packed[:, :half], bits[1:] + bits[:1]), (packed[:, half:], bits[:0:-1] + bits[:1])]
    held = [value[None] for value, _ in sides]
    orders = [[0], [0]]
    stages = []
    for k in range(len(bits)):
        before = tuple(held)
        for side, (_, path) in enumerate(sides):
            came = swapped(held[side], "seq", path[k])
            held[side] = jnp.concatenate([held[side], came])
            orders[side] = orders[side] + [o ^ path[k] for o in orders[side]]
        fill = [make(before) for make in beside[k : k + 1]]
        held = list(together(*held, *fill)[:2])
        stages.append(tuple(held))
    return held, orders, stages


def together(*values):
    return lax.optimization_barrier(values)


def tied(value, *others):
    return lax.optimization_barrier((value,) + others)[0]


def decay_table(held, order):
    logs = held[:, N, :384].astype(f32).reshape(-1, 3, 128).sum(axis=1)
    count = logs.shape[0]
    place = [order.index(k) for k in range(count)]
    return jnp.stack([logs[i] for i in place])


def joined_states(held, orders, logs, forward):
    count, mine = logs.shape[0], lax.axis_index("seq")
    who = jnp.arange(count) ^ mine
    if forward:
        counts = who < mine
        between = (who[None] > who[:, None]) & (who[None] < mine)
    else:
        counts = who > mine
        between = (who[None] < who[:, None]) & (who[None] > mine)
    power = jnp.sum(jnp.where(between[:, :, None], logs[None], 0.0), axis=1)
    factor = jnp.where(counts[:, None], jnp.exp2(power), 0.0)
    factor = jnp.repeat(factor[:, :H], P_SIZE, axis=1)
    half = E // 2
    sides = []
    for side in range(2):
        total = 0.0
        for i, k in enumerate(orders[side]):
            weight = factor[k, side * half : (side + 1) * half]
            total = total + weight[None] * held[side][i, :N].astype(f32)
        sides.append(total)
    return jnp.concatenate(sides, axis=1)


def cut(value, width, side):
    return lax.dynamic_slice_in_dim(value, side * width, width, 1)


def gathered(piece):
    return lax.all_gather(piece, "fsdp", axis=0, tiled=True)


def both_cores(mine):
    return mine, swapped(mine, "seq", 1)


def far_product(left, right, width, core):
    return tn(left, cut(right, width, 1 - core)).astype(bf16)


def half_product(left, right, width, core, came):
    return (tn(left, cut(right, width, core)) + came.astype(f32)).astype(bf16)


def part_sum(value):
    return lax.psum_scatter(value, "fsdp", scatter_dimension=0, tiled=True)


def added(value, bit):
    return (value.astype(f32) + swapped(value, "seq", bit).astype(f32)).astype(bf16)


def plane_step(first, second, k):
    bits = bits_of("seq")[1:]
    return added(first, bits[k]), added(second, bits[-1 - k])


def plane_sum(first, second):
    for k in range(len(bits_of("seq")) - 1):
        first, second = plane_step(first, second, k)
    return first, second


def swapped_pair(value):
    return value, swapped(value, "seq", 1)


def big_of(mine, other, core):
    def both(low, high):
        return ordered(mine[:, low:high], other[:, low:high], core)

    at = HZ + 2 * HD
    gate, conv = both(0, HZ), both(at, at + HX)
    tops, bottoms = both(HZ, HZ + HD), both(HZ + HD, at)
    steps = mine[:, at + HX : at + HX + H]
    return (
        jnp.concatenate([gate, conv, steps], axis=1).astype(f32),
        jnp.concatenate([tops, bottoms]).astype(f32),
    )


def plane_sum_rows(value):
    half = value.shape[0] // 2
    return jnp.concatenate(plane_sum(value[:half], value[half:]))


def ordered(mine, other, core):
    return jnp.concatenate(
        [jnp.where(core == 0, mine, other), jnp.where(core == 0, other, mine)], axis=1
    )


def reduced_small(value):
    parts, mine = lax.axis_size("fsdp"), lax.axis_index("fsdp")
    bit = parts // 2
    while bit:
        value = value.reshape((2, value.shape[0] // 2) + value.shape[1:])
        upper = (mine & bit) != 0
        kept = jnp.where(upper, value[1], value[0])
        value = kept + swapped(jnp.where(upper, value[0], value[1]), "fsdp", bit)
        bit //= 2
    for bit in bits_of("seq"):
        value = value + swapped(value, "seq", bit)
    return value[0]


def pad_lanes(value):
    return jnp.pad(value, ((0, 0), (0, 128 - value.shape[1])))


def token_table(doc, edge_ids):
    t = doc.shape[0]
    widened = jnp.concatenate([edge_ids, doc, jnp.full((K - 1,), -1, doc.dtype)])
    ids = [widened[k : k + t] == doc for k in range(K - 1)]
    ids += [widened[K - 1 + (K - 1 - k) :][:t] == doc for k in range(K - 1)]
    before = widened[K - 2 : K - 2 + t].reshape(t // Q, Q)[:, :1]
    blocks = doc.reshape(t // Q, Q)
    ids.append((blocks == before).reshape(t))
    ids.append((blocks == blocks[:, Q - 1 :]).reshape(t))
    cols_in = [v.astype(f32) for v in ids] + [doc.astype(f32)]
    table = pad_lanes(jnp.stack(cols_in, axis=1))
    return table, jnp.broadcast_to(doc.astype(f32)[None], (8, t))


def constants():
    spread = np.zeros((128, E), np.float32)
    for h in range(H):
        spread[h, h * P_SIZE : (h + 1) * P_SIZE] = 1
    hot = np.zeros((PAIRS, 2 * Q, 128), np.float32)
    sel = np.zeros((PAIRS, HP, 2 * Q), np.float32)
    for p in range(PAIRS):
        for i in range(2):
            hot[p, i * Q : (i + 1) * Q, 2 * p + i] = 1
            sel[p, 2 * p + i, i * Q : (i + 1) * Q] = 1
    return tuple(
        jnp.asarray(v, bf16) for v in (np.concatenate([spread, spread]), spread.T, hot, sel)
    )


SMALL = (K * CV, CV, H, H, H, D, E)


def local(
    first_tier_source,
    token_articles,
    extra_spikes,
    upstream_gradient,
    entering_projection,
    exit_projection,
    filter_kernels,
    filter_shifts,
    stride_shifts,
    log_shrink_rates,
    bypass_coefficient,
    entry_scaling_gains,
    gated_scaling_gains,
):
    current = first_tier_source[0]
    doc = token_articles[0]
    spike = pad_lanes(extra_spikes[0])
    t = doc.shape[0]
    layers = entering_projection.shape[0]
    parts = lax.axis_size("fsdp")
    e2, et, hot, sel = constants()
    edge_ids = passed_along(doc[t - (K - 1) :], "seq", 1)
    tok, doct = token_table(doc, edge_ids)

    small = (
        filter_kernels, filter_shifts, stride_shifts, log_shrink_rates, bypass_coefficient,
        entry_scaling_gains, gated_scaling_gains,
    )
    flat = jnp.concatenate([v.reshape(layers, -1) for v in small], axis=1)
    flat = lax.all_gather(flat, "fsdp").astype(f32)

    def small_of(layer):
        found, at = [], 0
        for size in SMALL:
            width = size // parts
            found.append(flat[:, layer, at : at + width])
            at += width
        taps = found[0].reshape(parts, K, CV // parts).transpose(1, 0, 2).reshape(K, CV)
        return [taps] + [v.reshape(-1) for v in found[1:]]

    core = lax.axis_index("seq") & 1
    cores = jnp.reshape(core, (1,)).astype(jnp.int32)
    bits = bits_of("seq")
    found = []
    for i in range(layers):
        w = entering_projection[i]
        steps = jnp.pad(w[:, E + CV :], ((0, 0), (0, 128 - H)))
        piece = jnp.concatenate([cut(w[:, E : E + CV], HX, core), steps], axis=1)
        gate, out = cut(w[:, :E], HZ, core), cut(exit_projection[i], HD, core)
        if i == 0:
            found.append((gathered(piece), gathered(gate), gathered(out)))
        else:
            rest = out.shape[0] // 2
            both = gathered(jnp.concatenate([gate, out[:rest], out[rest:]], axis=1))
            found.append((gathered(piece), both, None))
    weights = []
    kept = []
    for i in range(layers):
        wx = found[i][0]
        wx = both_cores(wx if i == 0 else tied(wx, current))
        taps, shifts, strides, rates, bypass, gain_in, gain_out = small_of(i)
        cw = jnp.concatenate([taps, shifts[None], jnp.zeros((3, CV), f32)])
        pv = jnp.concatenate(
            [pad_lanes(jnp.stack([strides, jnp.exp(rates)])), jnp.zeros((6, 128), f32)]
        )
        skip = jnp.repeat(bypass, P_SIZE)[None]
        gain_in, gain_out = gain_in[None], gain_out[None]
        normed, xc, dtr = project(cores, current, gain_in, *wx)
        edge = passed_along(xc[t - (K - 1) :], "seq", 1).astype(f32)
        edge = jnp.concatenate([jnp.zeros((8 - (K - 1), CV), f32), edge])
        pre, x, bc, dt, cum, cumt, dtt, packed = prepare(xc, edge, cw, dtr, spike, tok, pv, e2)
        yi = within(x, bc, cum, cumt, dtt, tok, doct)
        if i == 0:
            wz = both_cores(tied(found[i][1], x))
            made = []

            def gate_beside(before):
                made.append(project_gate(cores, tied(normed, *before), *wz))
                return made[0]

            held, orders, stages = all_states(packed, lambda before: yi, gate_beside)
            wo, z = both_cores(tied(found[i][2], *stages[1])), made[0]
        else:
            held, orders, stages = all_states(packed, lambda before: yi)
            both = tied(found[i][1], *stages[1])
            wz, wo = both[:, :HZ], both[:, HZ:].reshape(parts, -1, 2, HD)
            wo = wo.transpose(0, 2, 1, 3).reshape(E, HD)
            wz, wo = both_cores(wz), both_cores(wo)
            z = project_gate(cores, tied(normed, *stages[0]), *wz)
        weights.append((wx, wz, wo))
        logs = decay_table(held[0], orders[0])
        incoming = joined_states(held, orders, logs, True)
        out_type = bf16 if i == layers - 1 else f32
        y, low, new, prior = across(
            cores, yi, x, bc, dt, cum, tok, z, incoming, skip, gain_out, *wo, current, e2, out_type
        )
        kept.append(
            (current, normed, z, xc, dtr, edge, pre, x, bc, dt, cum, cumt, logs, y, low, prior,
             cw, pv, skip, gain_in, gain_out)
        )
        current = new
    grad = upstream_gradient[0]
    results = [None] * layers
    waiting = {}
    for i in reversed(range(layers)):
        wx, wz, wo = weights[i]
        (source, normed, z, xc, dtr, edge, pre, x, bc, dt, cum, cumt, logs, y, low, prior,
         cw, pv, skip, gain_in, gain_out) = kept[i]
        dy, dz, gb, acc, state = open_back(
            cores, grad, *wo, y, z, x, bc, cum, tok, gain_out, e2
        )
        far_gate = far_product(normed, dz, HZ, core)
        far_out = far_product(low, gb, HD, core)
        shared = (bc, dt, cum, cumt, tok, doct, hot, sel)
        near0 = within_back(tied(x, far_gate, far_out), dy, *shared, 0)
        top = waiting.get(i + 1)
        near1 = []

        def second_half(before):
            near1.extend(within_back(tied(x, near0[2], *before), dy, *shared, 1))
            return near1[2]

        came = (swapped(far_gate, "seq", 1), swapped(far_out, "seq", 1))
        held, orders, stages = all_states(state, lambda before: (near0[2], came), second_half)
        half_gate = half_product(normed, tied(dz, *stages[1]), HZ, core, came[0])
        half_out = half_product(low, tied(gb, *stages[1]), HD, core, came[1])
        grad_out, grad_gate = part_sum(half_out), part_sum(half_gate)
        later = joined_states(held, orders, logs, False)
        later = tied(later, half_out, half_gate)
        if top is not None:
            sums = added(tied(top, later), bits[1])
        dxc, cacc, hacc, first = across_back(
            x, pre, xc, edge, bc, dy, near0, near1, dt, cum, dtr, tok, prior, later, skip, cw, pv, e2, et
        )
        if top is not None:
            first, sums = together(first, sums)
        first, grad_out = together(first, grad_out)
        masked = [first[: K - 1] * tok[: K - 1, k : k + 1] for k in range(K - 1)]
        borrowed = jnp.stack(
            [sum(cw[k] * masked[k][e - k] for k in range(e + 1)) for e in range(K - 1)]
        )
        back = passed_along(borrowed, "seq", -1)
        gap = jnp.zeros((K - 1, 128), f32)
        back = jnp.concatenate([back[:, :HX], gap, back[:, HX:], gap], axis=1)
        mended = (dxc[t - (K - 1) :].astype(f32) + back).astype(bf16)
        dxc = dxc.at[t - (K - 1) :].set(mended)
        dxc, grad_gate = together(dxc, grad_gate)
        far_conv = far_product(normed, dxc, CX, core)
        conv_half = half_product(normed, dxc, CX, core, swapped(far_conv, "seq", 1))
        rest = grad_out.shape[0] // 2
        grad_out = jnp.concatenate([grad_out[:rest], grad_out[rest:]], axis=1)
        if i == 0:
            early = plane_sum(*tied((grad_gate, grad_out), far_conv))
            if top is not None:
                for bit in bits[2:]:
                    sums = added(sums, bit)
                grad = tied(grad, sums)
                results[i + 1] += (swapped_pair(sums),)
            grad = tied(grad, conv_half, *early)
            early = swapped_pair(jnp.concatenate(early, axis=1))
        grad, nacc = close_back(cores, dz, dxc, wz, wx, source, gain_in, grad)
        grad_conv = part_sum(conv_half)
        if i > 0:
            grad = tied(grad, conv_half)
            waiting[i] = jnp.concatenate([grad_gate, grad_out, grad_conv], axis=1)
        tiny = [
            cacc[:K], cacc[K], hacc[0, :H], hacc[1, :H],
            jnp.sum(acc[1].reshape(H, P_SIZE), axis=1), nacc[0], acc[0],
        ]
        results[i] = (tiny,)
    packed = []
    for i in range(layers):
        tiny = results[i][0]
        taps = tiny[0].reshape(K, parts, CV // parts).transpose(1, 0, 2).reshape(parts, -1)
        packed.append(jnp.concatenate([taps] + [v.reshape(parts, -1) for v in tiny[1:]], axis=1))
    mine = reduced_small(tied(jnp.stack(packed, axis=1), grad_conv))
    late = swapped_pair(plane_sum_rows(grad_conv))
    results[0] += (tuple(jnp.concatenate(v, axis=1) for v in zip(early, late)),)
    bigs = [
        big_of(*(tied(results[i][1], grad_conv) if i else results[i][1]), core)
        for i in range(layers)
    ]
    smalls, at = [], 0
    for size in SMALL:
        width = size // parts
        smalls.append(mine[:, at : at + width])
        at += width
    smalls[0] = smalls[0].reshape(layers, K, CV // parts)
    bigs = [jnp.stack([v[j] for v in bigs]) for j in range(2)]
    return (current[None], grad[None], *bigs, *smalls)


def solution(mesh):
    placed = (
        P("fsdp", "seq", None),
        P("fsdp", "seq"),
        P("fsdp", "seq", None),
        P("fsdp", "seq", None),
        P(None, "fsdp", None),
        P(None, "fsdp", None),
        P(None, None, "fsdp"),
        P(None, "fsdp"),
        P(None, "fsdp"),
        P(None, "fsdp"),
        P(None, "fsdp"),
        P(None, "fsdp"),
        P(None, "fsdp"),
    )
    return jax.shard_map(
        local,
        mesh=mesh,
        in_specs=placed,
        out_specs=(
            P("fsdp", "seq", None),
            P("fsdp", "seq", None),
            P(None, "fsdp", None),
            P(None, "fsdp", None),
            P(None, None, "fsdp"),
            P(None, "fsdp"),
            P(None, "fsdp"),
            P(None, "fsdp"),
            P(None, "fsdp"),
            P(None, "fsdp"),
            P(None, "fsdp"),
        ),
        check_vma=False,
    )
```
